128 devices in a mesh: dom: 128 (over y, z, x, core).
Axes of the slice: x: 4, y: 4, z: 4, core: 2. Of those that a mesh axis runs over, the one named last changes fastest.
Arguments:
- right_side: float32 [8, 2097152], P(None, 'dom'), may hold values from -24 to 24, as said below
- stiffness: float32 [3, 125, 32768], P(None, None, 'dom'), may hold values from 0.005 to 0.05
- mass: float32 [125, 32768], P(None, 'dom'), may hold values from 0.5 to 2
- region: int32 [32768], P('dom'), may hold values from 0 to 2
- density: float32 [3], replicated, may hold values from 0.5 to 2
- elem_nodes: int32 [125, 32768], P(None, 'dom'), may hold values from 0 to 32767, as said below
- peer_rank: int32 [128, 5], P('dom'), may hold values from 0 to 127, as said below
- send_nodes: int32 [128, 5, 128], P('dom'), may hold values from 0 to 16383, as said below
Outputs:
- solution: float32 [8, 2097152], P(None, 'dom')
- residual: float32 [8, 2097152], P(None, 'dom')
The draws below stay inside these ranges and needn't reach their ends.
Inputs may be any that keep to these rules, and one draw needn't show every extreme that they name: `right_side`: A mean scale that rises along the partitions. `peer_rank`: the peers of partition r, in a drawn order: r + 1 and r - 1 modulo 128, and r XOR 2**k for 3 bit positions k between 1 and log2(128) - 1 that are the same for every partition, the highest one among them. Peers are mutual. `send_nodes`: repeats are possible within one list. `elem_nodes`: A value 16384 + s * 128 + c names slot c of what peer s shares with this partition. Elements 2 g and 2 g + 1 of a partition name own nodes only from 128 g to 128 g + 127, each of them at least once. List the received slots of a partition in the order of its peer_rank slots, slot c fastest, and repeat that list cyclically: for g < 64 the elements 2 g and 2 g + 1 also name exactly the entries g * 10 to (g + 1) * 10 - 1 of it, each once; other elements name no received slot.
All inputs are finite; a program needn't handle non-finite values.
Results may differ from the reference program's by a relative error of at most 0.0003.
Values sent between devices are 32-bit elements; how exact they have to be, the bound alone decides.
A program may use at most 128 MiB of HBM per device.

```python
import math
import jax
import jax.numpy as jnp
import numpy as np
from jax import lax

NV = 8
NPE = 125
ELEM_DEV = 256
BND_DEV = 128
NODE_DEV = 16384
CAP = 128
NXOR = 3
NPEER = 5
GHOST_RUN = 10
ITERS = 2
ELEMS = 32768
NODES = 2097152
N_DOM = 128


def peer_table(key):
    levels = N_DOM.bit_length() - 1
    inner_bits = jax.random.permutation(jax.random.fold_in(key, 11), levels - 2).astype(jnp.int32) + 1
    bit_list = jnp.concatenate([inner_bits[:NXOR - 1], jnp.array([levels - 1], jnp.int32)])
    rank_list = jnp.arange(N_DOM, dtype=jnp.int32)
    columns = [(rank_list + 1) % N_DOM, (rank_list + N_DOM - 1) % N_DOM]
    for position in range(NXOR):
        columns.append(jnp.bitwise_xor(rank_list, jnp.left_shift(jnp.int32(1), bit_list[position])))
    peer_grid = jnp.stack(columns, axis=1).astype(jnp.int32)
    slot_keys = jax.random.split(jax.random.fold_in(key, 12), N_DOM)
    slot_order = jax.vmap(lambda slot_key: jax.random.permutation(slot_key, NPEER))(slot_keys).astype(jnp.int32)
    return jnp.take_along_axis(peer_grid, slot_order, axis=1).astype(jnp.int32)


def draw_peer_rank(key, part):
    return peer_table(key)


def draw_send_nodes(key, part):
    lists = jax.random.randint(jax.random.fold_in(key, 21), (N_DOM, NPEER, CAP), 0, NODE_DEV, dtype=jnp.int32)
    lists = lists.at[0, 0, 0].set(0)
    return lists.at[N_DOM - 1, NPEER - 1, CAP - 1].set(NODE_DEV - 1)


def draw_elem_nodes(key, part):
    peers = peer_table(key)
    pair_total = ELEM_DEV // 2
    edge_pairs = BND_DEV // 2
    window = NODE_DEV // pair_total
    live = NPEER * CAP

    def one_device(device_key, peer_row):
        slot_range = jnp.arange(CAP, dtype=jnp.int32)
        ghost_pool = (NODE_DEV + peer_row[:, None] * CAP + slot_range[None, :]).reshape(-1).astype(jnp.int32)
        runs = jnp.take(ghost_pool, jnp.arange(edge_pairs * GHOST_RUN, dtype=jnp.int32) % live).reshape(edge_pairs, GHOST_RUN)

        def edge_pair(pair_index, run):
            pair_key = jax.random.fold_in(device_key, pair_index)
            fill = jax.random.randint(jax.random.fold_in(pair_key, 1), (2 * NPE - GHOST_RUN - window,), 0, window, dtype=jnp.int32)
            own = pair_index * window + jnp.concatenate([jnp.arange(window, dtype=jnp.int32), fill])
            refs = jax.random.permutation(jax.random.fold_in(pair_key, 2), jnp.concatenate([own, run]))
            return refs.reshape(2, NPE).T

        def inner_pair(pair_index):
            pair_key = jax.random.fold_in(device_key, pair_index)
            fill = jax.random.randint(jax.random.fold_in(pair_key, 1), (2 * NPE - window,), 0, window, dtype=jnp.int32)
            own = pair_index * window + jnp.concatenate([jnp.arange(window, dtype=jnp.int32), fill])
            refs = jax.random.permutation(jax.random.fold_in(pair_key, 2), own)
            return refs.reshape(2, NPE).T
        edge_blocks = jax.vmap(edge_pair)(jnp.arange(edge_pairs, dtype=jnp.int32), runs)
        inner_blocks = jax.vmap(inner_pair)(jnp.arange(edge_pairs, pair_total, dtype=jnp.int32))
        all_pairs = jnp.concatenate([edge_blocks, inner_blocks], axis=0)
        return jnp.transpose(all_pairs, (1, 0, 2)).reshape(NPE, ELEM_DEV).astype(jnp.int32)
    device_keys = jax.random.split(jax.random.fold_in(key, 31), N_DOM)
    blocks = jax.vmap(one_device)(device_keys, peers)
    return jnp.transpose(blocks, (1, 0, 2)).reshape(NPE, N_DOM * ELEM_DEV).astype(jnp.int32)


def draw_right_side(key, part):
    node_ids = jnp.arange(NODES, dtype=jnp.int32)
    device_of = (node_ids // NODE_DEV).astype(jnp.float32)
    rising = jnp.exp(jnp.log(3.0) * device_of / (N_DOM - 1))
    values = jnp.clip(jax.random.normal(key, (NV, NODES), jnp.float32), -5.0, 5.0) * rising[None, :]
    return values


def with_ends(values, key, smallest, largest):
    spot = [jax.random.randint(jax.random.fold_in(key, axis), (), 0, length) for axis, length in enumerate(values.shape)]
    longest = values.shape.index(max(values.shape))
    beside = spot[:longest] + [(spot[longest] + 1) % values.shape[longest]] + spot[longest + 1:]
    return values.at[tuple(spot)].set(smallest).at[tuple(beside)].set(largest)


def steps_of(rng, extent, shards, least, high):
    factor_of = 1.0
    for dim, shards_of in shards:
        heights = jax.random.uniform(jax.random.fold_in(jax.random.fold_in(rng, 6), dim), (shards_of,), jnp.float32, least / len(shards), high / len(shards))
        factor_of = factor_of * jnp.repeat(jnp.exp(heights), extent[dim] // shards_of).reshape((-1,) + (1,) * (len(extent) - 1 - dim))
    return factor_of


def setup_inputs(seed: int = 0) -> dict:
    key_list = jax.random.split(jax.random.key(seed), 9)
    right_side = draw_right_side(jax.random.fold_in(key_list[8], 71), 0)
    stiffness = jnp.clip(jnp.exp(math.log(0.05) - 2.3025851 * jax.random.uniform(key_list[1], (3, NPE, ELEMS), jnp.float32) ** steps_of(key_list[1], (3, NPE, ELEMS), ((2, 128),), -0.2, 0.2)), 0.005, 0.05)
    mass = jnp.clip(jnp.exp(math.log(2.0) - 1.3862944 * jax.random.uniform(key_list[2], (NPE, ELEMS), jnp.float32) ** steps_of(key_list[2], (NPE, ELEMS), ((1, 128),), -0.2, 0.2)), 0.5, 2.0)
    region = with_ends(jax.random.randint(key_list[3], (ELEMS,), 0, 3), jax.random.fold_in(key_list[3], 1), 0, 2).astype(jnp.int32)
    density = jnp.clip(jnp.exp(jax.random.uniform(key_list[4], (3,), jnp.float32, math.log(0.5), math.log(2.0))), 0.5, 2.0)
    elem_nodes = draw_elem_nodes(jax.random.fold_in(key_list[8], 71), 0)
    peer_rank = draw_peer_rank(jax.random.fold_in(key_list[8], 71), 0)
    send_nodes = draw_send_nodes(jax.random.fold_in(key_list[8], 71), 0)
    return {"right_side": right_side, "stiffness": stiffness, "mass": mass, "region": region, "density": density, "elem_nodes": elem_nodes, "peer_rank": peer_rank, "send_nodes": send_nodes}


precise = lax.Precision.HIGHEST

def gll_matrix():
    points = np.array([-1.0, -np.sqrt(3.0 / 7.0), 0.0, np.sqrt(3.0 / 7.0), 1.0])
    weights = np.array([1.0 / np.prod([points[column] - points[other] for other in range(5) if other != column]) for column in range(5)])
    matrix = np.zeros((5, 5))
    for row_index in range(5):
        for column in range(5):
            if row_index != column:
                matrix[row_index, column] = weights[column] / weights[row_index] / (points[row_index] - points[column])
        matrix[row_index, row_index] = -np.sum(matrix[row_index])
    return matrix

def element_apply(gathered, stiff_grid, mass_grid, derivative):
    grad_first = jnp.einsum('ai,vijke->vajke', derivative, gathered, precision=precise)
    result = jnp.einsum('ai,vajke->vijke', derivative, stiff_grid[0] * grad_first, precision=precise)
    grad_second = jnp.einsum('bj,vijke->vibke', derivative, gathered, precision=precise)
    result = result + jnp.einsum('bj,vibke->vijke', derivative, stiff_grid[1] * grad_second, precision=precise)
    grad_third = jnp.einsum('ck,vijke->vijce', derivative, gathered, precision=precise)
    result = result + jnp.einsum('ck,vijce->vijke', derivative, stiff_grid[2] * grad_third, precision=precise)
    return result + mass_grid * gathered

def element_diagonal(stiff_grid, mass_grid, derivative):
    square = derivative * derivative
    first = jnp.einsum('ai,ajke->ijke', square, stiff_grid[0], precision=precise)
    second = jnp.einsum('bj,ibke->ijke', square, stiff_grid[1], precision=precise)
    third = jnp.einsum('ck,ijce->ijke', square, stiff_grid[2], precision=precise)
    return first + second + third + mass_grid

def reference(right_side, stiffness, mass, region, density, elem_nodes, peer_rank, send_nodes):
    derivative = jnp.asarray(gll_matrix(), jnp.float32)
    sources = jnp.broadcast_to(jnp.arange(N_DOM, dtype=jnp.int32)[:, None], peer_rank.shape)
    offsets = (jnp.arange(N_DOM, dtype=jnp.int32)[:, None, None] * NODE_DEV + send_nodes).astype(jnp.int32)
    table = jnp.zeros((N_DOM, N_DOM, CAP), jnp.int32).at[peer_rank, sources].set(offsets)
    table = table.reshape(N_DOM, N_DOM * CAP)
    blocks = elem_nodes.reshape(NPE, N_DOM, ELEM_DEV).transpose(1, 0, 2)

    def globalize(device, block_list, table_row):
        own_global = device * NODE_DEV + block_list
        remote = jnp.take(table_row, jnp.clip(block_list - NODE_DEV, 0, N_DOM * CAP - 1))
        return jnp.where(block_list < NODE_DEV, own_global, remote).astype(jnp.int32)
    global_nodes = jax.vmap(globalize)(jnp.arange(N_DOM, dtype=jnp.int32), blocks, table)
    mass_term = jnp.take(density, region)[None, :] * mass
    diag_terms = element_diagonal(stiffness.reshape(3, 5, 5, 5, ELEMS), mass_term.reshape(5, 5, 5, ELEMS), derivative)
    diag_terms = diag_terms.reshape(NPE, N_DOM, ELEM_DEV).transpose(1, 0, 2)
    diagonal = jnp.zeros((NODES,), jnp.float32).at[global_nodes.reshape(-1)].add(diag_terms.reshape(-1))

    def operator(vector_field):

        def one_block(device, summed):
            node_list = lax.dynamic_index_in_dim(global_nodes, device, 0, keepdims=False).reshape(-1)
            start = (device * ELEM_DEV).astype(jnp.int32)
            stiff_grid = lax.dynamic_slice_in_dim(stiffness, start, ELEM_DEV, 2).reshape(3, 5, 5, 5, ELEM_DEV)
            mass_block = lax.dynamic_slice_in_dim(mass_term, start, ELEM_DEV, 1).reshape(5, 5, 5, ELEM_DEV)
            gathered = jnp.take(vector_field, node_list, axis=1).reshape(NV, 5, 5, 5, ELEM_DEV)
            result = element_apply(gathered, stiff_grid, mass_block, derivative)
            return summed.at[:, node_list].add(result.reshape(NV, -1))
        return lax.fori_loop(0, N_DOM, one_block, jnp.zeros_like(vector_field))
    solution = jnp.zeros_like(right_side)
    residual = right_side
    precond = residual / diagonal[None, :]
    direction = precond
    product_now = lax.optimization_barrier(jnp.sum(residual * precond, axis=1))
    for iteration in range(ITERS):
        applied = operator(direction)
        step_size = product_now / lax.optimization_barrier(jnp.sum(direction * applied, axis=1))
        solution = solution + step_size[:, None] * direction
        residual = residual - step_size[:, None] * applied
        precond = residual / diagonal[None, :]
        product_next = lax.optimization_barrier(jnp.sum(residual * precond, axis=1))
        direction = precond + (product_next / product_now)[:, None] * direction
        product_now = product_next
    return (solution, residual)
```

```python
import functools

import jax
import jax.numpy as jnp
import numpy as np
from jax import lax
from jax.experimental import pallas as pl
from jax.experimental.pallas import tpu as pltpu
from jax.sharding import PartitionSpec as P

MESH = pl.DeviceIdType.MESH
F32 = jnp.float32
BF16 = jnp.bfloat16
NV = 8
NPE = 125
LANES = 128
GROUP = 8
KEYS = 144
BLOCK = 16


def gll_matrix():
    points = np.array([-1.0, -np.sqrt(3.0 / 7.0), 0.0, np.sqrt(3.0 / 7.0), 1.0])
    weights = np.array(
        [
            1.0 / np.prod([points[column] - points[other] for other in range(5) if other != column])
            for column in range(5)
        ]
    )
    matrix = np.zeros((5, 5))
    for row_index in range(5):
        for column in range(5):
            if row_index != column:
                matrix[row_index, column] = (
                    weights[column] / weights[row_index] / (points[row_index] - points[column])
                )
        matrix[row_index, row_index] = -np.sum(matrix[row_index])
    return matrix


def split_numpy(matrix):
    single = matrix.astype(np.float32)
    high = single.astype(jnp.bfloat16)
    low = (single - high.astype(np.float32)).astype(jnp.bfloat16)
    return high, low


def operator_matrices():
    matrix = gll_matrix().astype(np.float32)
    eye = np.eye(5, dtype=np.float32)

    def along(small):
        full = np.zeros((3, LANES, LANES), np.float32)
        full[0, :NPE, :NPE] = np.kron(np.kron(small, eye), eye)
        full[1, :NPE, :NPE] = np.kron(np.kron(eye, small), eye)
        full[2, :NPE, :NPE] = np.kron(np.kron(eye, eye), small)
        return full

    grad = np.concatenate([full.T for full in along(matrix)], axis=1)
    first_high, first_low = split_numpy(grad)
    first = np.concatenate([first_high, first_low], axis=1)
    first = np.concatenate([first, first], axis=0)
    back = np.concatenate(list(along(matrix)), axis=0)
    second = np.concatenate(split_numpy(back), axis=1)
    second = np.concatenate([second, second], axis=0)
    square = np.concatenate(list(along(matrix * matrix)), axis=0)
    third = np.concatenate(split_numpy(square), axis=1)
    third = np.concatenate([third, third], axis=0)
    return first, second, third


def split(value):
    high = value.astype(BF16)
    return high, (value - high.astype(F32)).astype(BF16)


def parts(value):
    return jnp.concatenate(split(value), axis=1)


def matmul(left, right):
    return lax.dot_general(left, right, (((1,), (0,)), ((), ())), preferred_element_type=F32)


def matmul_nt(left, right):
    return lax.dot_general(left, right, (((1,), (1,)), ((), ())), preferred_element_type=F32)


def flipped(rank, bit):
    return rank + bit - 2 * bit * ((rank // bit) % 2)


def kernel(
    devices,
    density,
    peer_rank,
    right,
    stiffness,
    mass,
    region,
    nodes,
    send_nodes,
    first,
    second,
    third,
    solution_out,
    residual_out,
    stiff,
    mass_term,
    node_table,
    key_table,
    hot,
    diag_term,
    diagonal,
    z_own,
    w_own,
    q_own,
    p_own,
    lane_hot,
    lane_hot_t,
    values,
    ghost,
    compact,
    outgoing,
    incoming_0,
    incoming_1,
    incoming_2,
    incoming_3,
    incoming_4,
    ordered,
    send_sem,
    recv_sem,
    partial,
    near_in,
    far_in,
    near_send,
    near_recv,
    far_send,
    far_recv,
):
    me = lax.axis_index("dom")
    incoming = [incoming_0, incoming_1, incoming_2, incoming_3, incoming_4]
    elems = nodes.shape[1]
    pairs = elems // 2
    edge_pairs = pairs // 2
    peers = send_nodes.shape[1]
    live = peers * LANES
    run = live // edge_pairs
    bits = devices.bit_length() - 1
    candidates = [(me + 1) % devices, (me + devices - 1) % devices]
    candidates += [flipped(me, 2**k) for k in range(1, bits)]
    arrival = [1, 0] + list(range(2, len(candidates)))
    far_count = devices // GROUP
    near = [me - me % GROUP + (me + step) % GROUP for step in range(1, GROUP)]
    far = [(me + step * GROUP) % devices for step in range(1, far_count)]

    barrier = pltpu.get_barrier_semaphore()
    for other in candidates + near + far:
        pl.semaphore_signal(barrier, inc=1, device_id=(other,), device_id_type=MESH)

    stiff[...] = jnp.zeros_like(stiff)
    mass_term[...] = jnp.zeros_like(mass_term)
    node_table[...] = jnp.zeros_like(node_table)
    lane_row = lax.broadcasted_iota(jnp.int32, (1, LANES), 1)
    for half in range(elems // LANES):
        columns = slice(half * LANES, (half + 1) * LANES)
        for axis in range(3):
            stiff[columns, axis * LANES : axis * LANES + NPE] = stiffness[axis, :, columns].T
        tag = region[:, columns]
        weight = jnp.where(
            tag == 0, density[0], jnp.where(tag == 1, density[1], density[2])
        )
        mass_term[columns, :NPE] = (mass[:, columns] * weight).T
        node_table[columns, :NPE] = nodes[:, columns].T
    table = node_table[...]
    own_count = pairs * LANES
    pair_of = lax.broadcasted_iota(jnp.int32, table.shape, 0) // 2
    key = jnp.where(
        table < own_count, table & (LANES - 1), LANES + ((table - run * pair_of) & (LANES - 1))
    )
    key_table[...] = jnp.where(
        lax.broadcasted_iota(jnp.int32, table.shape, 1) < NPE, key, 255
    )
    sends = send_nodes[0]
    send_row = jnp.concatenate([sends[p : p + 1, :] for p in range(peers)], axis=1)
    send_lane = send_row & (LANES - 1)
    send_window = jnp.broadcast_to(send_row // LANES, (NV, live))
    picks = (
        lax.broadcasted_iota(jnp.int32, (LANES, live), 0) == send_lane
    ).astype(F32).astype(BF16)
    lane_hot[:LANES] = picks
    lane_hot[LANES:] = picks
    lane_hot_t[:, :live] = picks
    lane_hot_t[:, live:] = picks
    ghost[...] = jnp.zeros_like(ghost)

    diag_out = matmul(parts(stiff[...]), third[...])
    diag_term[...] = diag_out[:, :LANES] + diag_out[:, LANES:] + mass_term[...]

    def scatter_pair(pair, both):
        rows = jnp.concatenate([both, both - both.astype(BF16).astype(F32)], axis=0).astype(BF16)
        summed = matmul_nt(rows, hot[pair])
        return summed[:NV] + summed[NV:]

    def gather_ghosts():
        slots = [jnp.zeros((NV, LANES), F32) for _ in range(peers)]
        lane = lax.broadcasted_iota(jnp.int32, (NV, LANES), 1)
        for pair in range(edge_pairs):
            base = pair * run
            begin = base % LANES
            row = ghost[pair]
            if begin:
                row = pltpu.roll(row, begin, 1)
            here, last = base // LANES, (base + run - 1) // LANES
            if here == last:
                slots[here] = slots[here] + row
            else:
                slots[here] = slots[here] + jnp.where(lane >= begin, row, 0.0)
                slots[last] = slots[last] + jnp.where(lane < begin, row, 0.0)
        return slots

    def remote(phase, j):
        return pltpu.make_async_remote_copy(
            src_ref=outgoing.at[phase, j],
            dst_ref=incoming[phase].at[arrival[j]],
            send_sem=send_sem.at[phase, j],
            recv_sem=recv_sem.at[phase, arrival[j]],
            device_id=(candidates[j],),
            device_id_type=MESH,
        )

    def slot_of(j):
        slot = jnp.int32(0)
        for p in range(peers):
            slot = jnp.where(peer_rank[0, p] == candidates[j], p, slot)
        return slot

    def candidate_of(p):
        found = jnp.int32(0)
        for j in range(len(candidates)):
            found = jnp.where(peer_rank[0, p] == candidates[j], j, found)
        return found

    slots_of = [slot_of(j) for j in range(len(candidates))]
    candidates_of = [candidate_of(p) for p in range(peers)]

    def send(phase, slots):
        for p in range(peers):
            compact[phase, p] = slots[p]
        for j in range(len(candidates)):
            outgoing[phase, j] = compact[phase, slots_of[j]]
            remote(phase, j).start()

    def receive(phase):
        for j in range(len(candidates)):
            remote(phase, j).wait_recv()
        return [incoming[phase][candidates_of[p]] for p in range(peers)]

    def add_returned(own, received):
        value = jnp.concatenate(received, axis=1)

        def body(block, carry):
            rows = []
            for i in range(BLOCK):
                rows.append(jnp.where(send_window == block * BLOCK + i, value, 0.0))
            picked = parts(jnp.concatenate(rows, axis=0))
            at = pl.ds(pl.multiple_of(block * BLOCK * NV, BLOCK * NV), BLOCK * NV)
            own[at, :] = own[at, :] + matmul_nt(picked, lane_hot_t[...])
            return carry

        lax.fori_loop(0, pairs // BLOCK, body, 0)

    def pick_shared(own):
        def body(block, total):
            at = pl.ds(pl.multiple_of(block * BLOCK * NV, BLOCK * NV), BLOCK * NV)
            spread = matmul(parts(own[at, :]), lane_hot[...])
            for i in range(BLOCK):
                total = total + jnp.where(
                    send_window == block * BLOCK + i, spread[i * NV : (i + 1) * NV], 0.0
                )
            return total

        total = lax.fori_loop(0, pairs // BLOCK, body, jnp.zeros((NV, live), F32))
        return [total[:, p * LANES : (p + 1) * LANES] for p in range(peers)]

    def build_and_scatter(edge):
        def body(index, carry):
            pair = index if edge else index + edge_pairs
            count = KEYS if edge else LANES
            both = pl.ds(2 * pair, 1), pl.ds(2 * pair + 1, 1)
            keys = jnp.concatenate([key_table[both[0], :], key_table[both[1], :]], axis=1)
            rows = lax.broadcasted_iota(jnp.int32, (count, 2 * LANES), 0)
            hot[pair, :count] = (rows == keys).astype(F32).astype(BF16)
            term = jnp.concatenate([diag_term[both[0], :], diag_term[both[1], :]], axis=1)
            summed = scatter_pair(pair, jnp.broadcast_to(term, (NV, 2 * LANES)))
            at = pl.ds(pl.multiple_of(pair * NV, NV), NV)
            diagonal[at, :] = summed[:, :LANES]
            if edge:
                ghost[pair, :, : KEYS - LANES] = summed[:, LANES:]
            return carry

        lax.fori_loop(0, edge_pairs, body, 0, unroll=4)

    def apply_blocks(source, target, edge, total):
        def body(index, total):
            block = index if edge else index + edge_pairs // BLOCK
            for i in range(BLOCK):
                pair = block * BLOCK + i
                own = source[pl.ds(pl.multiple_of(pair * NV, NV), NV), :]
                if edge:
                    base = pair * run
                    lane = lax.broadcasted_iota(jnp.int32, (NV, LANES), 1)
                    begin = base % LANES
                    received = jnp.where(
                        lane >= begin, ordered[base // LANES], ordered[(base + run - 1) // LANES]
                    )
                for side in range(2):
                    node = jnp.broadcast_to(node_table[pl.ds(2 * pair + side, 1), :], (NV, LANES))
                    lanes = node & (LANES - 1)
                    picked = jnp.take_along_axis(own, lanes, axis=1, mode="promise_in_bounds")
                    if edge:
                        remote_value = jnp.take_along_axis(
                            received, lanes, axis=1, mode="promise_in_bounds"
                        )
                        picked = jnp.where(node < own_count, picked, remote_value)
                    values[(2 * i + side) * NV : (2 * i + side + 1) * NV, :] = picked
            value = values[...]
            grad = matmul(parts(value), first[...])
            flux = grad[:, : 3 * LANES] + grad[:, 3 * LANES :]
            scaled = []
            masses = []
            for i in range(2 * BLOCK):
                at = pl.ds(block * 2 * BLOCK + i, 1)
                scaled.append(flux[i * NV : (i + 1) * NV] * stiff[at, :])
                masses.append(jnp.broadcast_to(mass_term[at, :], (NV, LANES)))
            back = matmul(parts(jnp.concatenate(scaled, axis=0)), second[...])
            result = back[:, :LANES] + back[:, LANES:] + jnp.concatenate(masses, axis=0) * value
            product = value * result
            for i in range(2 * BLOCK):
                total = total + product[i * NV : (i + 1) * NV]
            for i in range(BLOCK):
                pair = block * BLOCK + i
                low = 2 * i * NV
                both = jnp.concatenate(
                    [result[low : low + NV], result[low + NV : low + 2 * NV]], axis=1
                )
                rows = jnp.concatenate(
                    [both, both - both.astype(BF16).astype(F32)], axis=0
                ).astype(BF16)
                count = KEYS if edge else LANES
                summed = matmul_nt(rows, hot[pair, :count])
                summed = summed[:NV] + summed[NV:]
                target[pl.ds(pl.multiple_of(pair * NV, NV), NV), :] = summed[:, :LANES]
                if edge:
                    ghost[pair, :, : KEYS - LANES] = summed[:, LANES:]
            return total

        return lax.fori_loop(0, edge_pairs // BLOCK, body, total)

    def over_pairs(step, total):
        def body(pair, total):
            return step(pair, pl.ds(pl.multiple_of(pair * NV, NV), NV), total)

        return lax.fori_loop(0, pairs, body, total, unroll=8)

    zero = jnp.zeros((NV, LANES), F32)
    build_and_scatter(True)
    pl.semaphore_wait(barrier, len(candidates) + len(near) + len(far))
    send(0, gather_ghosts())
    build_and_scatter(False)
    add_returned(diagonal, receive(0))

    def begin(pair, at, total):
        value = right[:, pl.ds(pl.multiple_of(pair * LANES, LANES), LANES)]
        scaled = value / diagonal[at, :]
        z_own[at, :] = scaled
        return total + value * scaled

    sum_rz = over_pairs(begin, zero)

    def apply(source, target, phase):
        send(phase, pick_shared(source))
        total = apply_blocks(source, target, False, zero)
        for p, value in enumerate(receive(phase)):
            ordered[p] = value
        total = apply_blocks(source, target, True, total)
        send(phase + 1, gather_ghosts())
        return total

    sum_zw = apply(z_own, w_own, 1)
    add_returned(w_own, receive(2))

    def middle(pair, at, total):
        value = w_own[at, :]
        scaled = value / diagonal[at, :]
        q_own[at, :] = scaled
        return total + value * scaled

    sum_wq = over_pairs(middle, zero)
    sum_qp = apply(q_own, p_own, 3)

    lane = lax.broadcasted_iota(jnp.int32, (NV, LANES), 1)
    quarter = LANES // 4
    packed = zero
    for place, total in enumerate((sum_rz, sum_zw, sum_wq, sum_qp)):
        total = total + pltpu.roll(total, LANES // 2, 1)
        total = total + pltpu.roll(total, quarter, 1)
        packed = jnp.where(lane // quarter == place, total, packed)

    def near_copy(step):
        return pltpu.make_async_remote_copy(
            src_ref=partial.at[0],
            dst_ref=near_in.at[step],
            send_sem=near_send.at[step],
            recv_sem=near_recv.at[step],
            device_id=(near[step],),
            device_id_type=MESH,
        )

    def far_copy(step):
        return pltpu.make_async_remote_copy(
            src_ref=partial.at[1],
            dst_ref=far_in.at[step],
            send_sem=far_send.at[step],
            recv_sem=far_recv.at[step],
            device_id=(far[step],),
            device_id_type=MESH,
        )

    partial[0] = packed
    for step in range(len(near)):
        near_copy(step).start()
    for step in range(len(near)):
        near_copy(step).wait_recv()
        packed = packed + near_in[step]
    partial[1] = packed
    for step in range(len(far)):
        far_copy(step).start()
    add_returned(p_own, receive(4))
    for step in range(len(far)):
        far_copy(step).wait_recv()
        packed = packed + far_in[step]
    rz, zw, wq, qp = [
        jnp.sum(jnp.where(lane // quarter == place, packed, 0.0), axis=1, keepdims=True)
        for place in range(4)
    ]
    alpha = rz / zw
    new = rz - 2.0 * alpha * zw + alpha * alpha * wq
    ratio = 1.0 + new / rz
    second_alpha = new / (
        ratio * ratio * zw - 2.0 * alpha * ratio * wq + alpha * alpha * qp
    )
    outer = jnp.broadcast_to(alpha + second_alpha * ratio, (NV, LANES))
    inner = jnp.broadcast_to(alpha * second_alpha, (NV, LANES))

    def finish(pair, at, total):
        out = pl.ds(pl.multiple_of(pair * LANES, LANES), LANES)
        solution_out[:, out] = outer * z_own[at, :] - inner * q_own[at, :]
        residual_out[:, out] = right[:, out] - outer * w_own[at, :] + inner * p_own[at, :]
        return total

    over_pairs(finish, zero)
    for phase in range(5):
        for j in range(len(candidates)):
            remote(phase, j).wait_send()
    for step in range(len(near)):
        near_copy(step).wait_send()
    for step in range(len(far)):
        far_copy(step).wait_send()


def on_device(devices, right, stiffness, mass, region, density, elem_nodes, peer_rank, send_nodes):
    first, second, third = (jnp.asarray(matrix) for matrix in operator_matrices())
    own_count = right.shape[1]
    elems = elem_nodes.shape[1]
    pairs = elems // 2
    peers = send_nodes.shape[1]
    live = peers * LANES
    bits = devices.bit_length() - 1
    ways = bits + 1
    near_count, far_count = GROUP - 1, devices // GROUP - 1
    vmem = pl.BlockSpec(memory_space=pltpu.VMEM)
    smem = pl.BlockSpec(memory_space=pltpu.SMEM)
    owned = pltpu.VMEM((pairs * NV, LANES), F32)
    dma = pltpu.SemaphoreType.DMA
    return pl.pallas_call(
        functools.partial(kernel, devices),
        out_shape=(
            jax.ShapeDtypeStruct((NV, own_count), F32),
            jax.ShapeDtypeStruct((NV, own_count), F32),
        ),
        in_specs=[smem, smem] + [vmem] * 9,
        out_specs=(vmem, vmem),
        scratch_shapes=[
            pltpu.VMEM((elems, 3 * LANES), F32),
            pltpu.VMEM((elems, LANES), F32),
            pltpu.VMEM((elems, LANES), jnp.int32),
            pltpu.VMEM((elems, LANES), jnp.int32),
            pltpu.VMEM((pairs, KEYS, 2 * LANES), BF16),
            pltpu.VMEM((elems, LANES), F32),
            owned,
            owned,
            owned,
            owned,
            owned,
            pltpu.VMEM((2 * LANES, live), BF16),
            pltpu.VMEM((LANES, 2 * live), BF16),
            pltpu.VMEM((2 * BLOCK * NV, LANES), F32),
            pltpu.VMEM((pairs // 2, NV, LANES), F32),
            pltpu.VMEM((5, peers, NV, LANES), F32),
            pltpu.VMEM((5, ways, NV, LANES), F32),
            pltpu.VMEM((ways, NV, LANES), F32),
            pltpu.VMEM((ways, NV, LANES), F32),
            pltpu.VMEM((ways, NV, LANES), F32),
            pltpu.VMEM((ways, NV, LANES), F32),
            pltpu.VMEM((ways, NV, LANES), F32),
            pltpu.VMEM((peers, NV, LANES), F32),
            dma((5, ways)),
            dma((5, ways)),
            pltpu.VMEM((2, NV, LANES), F32),
            pltpu.VMEM((near_count, NV, LANES), F32),
            pltpu.VMEM((far_count, NV, LANES), F32),
            dma((near_count,)),
            dma((near_count,)),
            dma((far_count,)),
            dma((far_count,)),
        ],
        compiler_params=pltpu.CompilerParams(
            collective_id=0, has_side_effects=True, vmem_limit_bytes=48 * 1024 * 1024
        ),
    )(
        density,
        peer_rank,
        right,
        stiffness,
        mass,
        region.reshape(1, elems),
        elem_nodes,
        send_nodes,
        first,
        second,
        third,
    )


def solution(mesh):
    devices = mesh.shape["dom"]
    placed = (
        P(None, "dom"),
        P(None, None, "dom"),
        P(None, "dom"),
        P("dom"),
        P(),
        P(None, "dom"),
        P("dom", None),
        P("dom", None, None),
    )
    return jax.shard_map(
        functools.partial(on_device, devices),
        mesh=mesh,
        in_specs=placed,
        out_specs=(P(None, "dom"), P(None, "dom")),
        check_vma=False,
    )
```

```python
import functools

import jax
import jax.numpy as jnp
import numpy as np
from jax import lax
from jax.experimental import pallas as pl
from jax.experimental.pallas import tpu as pltpu
from jax.sharding import PartitionSpec as P

MESH = pl.DeviceIdType.MESH
F32 = jnp.float32
BF16 = jnp.bfloat16
NV = 8
NPE = 125
LANES = 128
GROUP = 8
KEYS = 144
BLOCK = 16
WIDE = 32


def gll_matrix():
    points = np.array([-1.0, -np.sqrt(3.0 / 7.0), 0.0, np.sqrt(3.0 / 7.0), 1.0])
    weights = np.array(
        [
            1.0 / np.prod([points[column] - points[other] for other in range(5) if other != column])
            for column in range(5)
        ]
    )
    matrix = np.zeros((5, 5))
    for row_index in range(5):
        for column in range(5):
            if row_index != column:
                matrix[row_index, column] = (
                    weights[column] / weights[row_index] / (points[row_index] - points[column])
                )
        matrix[row_index, row_index] = -np.sum(matrix[row_index])
    return matrix


def split_numpy(matrix):
    single = matrix.astype(np.float32)
    high = single.astype(jnp.bfloat16)
    low = (single - high.astype(np.float32)).astype(jnp.bfloat16)
    return high, low


def operator_matrices():
    matrix = gll_matrix().astype(np.float32)
    eye = np.eye(5, dtype=np.float32)

    def along(small):
        full = np.zeros((3, LANES, LANES), np.float32)
        full[0, :NPE, :NPE] = np.kron(np.kron(small, eye), eye)
        full[1, :NPE, :NPE] = np.kron(np.kron(eye, small), eye)
        full[2, :NPE, :NPE] = np.kron(np.kron(eye, eye), small)
        return full

    grad = np.concatenate([full.T for full in along(matrix)], axis=1)
    first_high, first_low = split_numpy(grad)
    first = np.concatenate([first_high, first_low], axis=1)
    first = np.concatenate([first, first], axis=0)
    back = np.concatenate(list(along(matrix)), axis=0)
    second = np.concatenate(split_numpy(back), axis=1)
    second = np.concatenate([second, second], axis=0)
    square = np.concatenate(list(along(matrix * matrix)), axis=0)
    third = np.concatenate(split_numpy(square), axis=1)
    third = np.concatenate([third, third], axis=0)
    return first, second, third


def split(value):
    high = value.astype(BF16)
    return high, (value - high.astype(F32)).astype(BF16)


def parts(value):
    return jnp.concatenate(split(value), axis=1)


def matmul(left, right):
    return lax.dot_general(left, right, (((1,), (0,)), ((), ())), preferred_element_type=F32)


def matmul_nt(left, right):
    return lax.dot_general(left, right, (((1,), (1,)), ((), ())), preferred_element_type=F32)


def flipped(rank, bit):
    return rank + bit - 2 * bit * ((rank // bit) % 2)


def kernel(
    devices,
    density,
    peer_rank,
    right_in,
    stiffness_in,
    mass_in,
    region_in,
    nodes_in,
    send_in,
    first_in,
    second_in,
    third_in,
    solution_out,
    residual_out,
    right,
    stiffness,
    mass,
    region,
    nodes,
    send_nodes,
    first,
    second,
    third,
    in_sem,
    stiff,
    mass_term,
    node_table,
    key_table,
    hot,
    diag_term,
    diagonal,
    z_own,
    w_own,
    q_own,
    p_own,
    lane_hot,
    back_hot,
    same_hot,
    diag_rows,
    ghost,
    compact,
    outgoing,
    incoming_0,
    incoming_1,
    incoming_2,
    incoming_3,
    incoming_4,
    ordered,
    send_sem,
    recv_sem,
    partial,
    near_in,
    far_in,
    near_send,
    near_recv,
    far_send,
    far_recv,
):
    me = lax.axis_index("dom")
    incoming = [incoming_0, incoming_1, incoming_2, incoming_3, incoming_4]
    elems = nodes.shape[1]
    pairs = elems // 2
    edge_pairs = pairs // 2
    peers = send_nodes.shape[0]
    live = peers * LANES
    run = live // edge_pairs
    bits = devices.bit_length() - 1
    candidates = [(me + 1) % devices, (me + devices - 1) % devices]
    candidates += [flipped(me, 2**k) for k in range(1, bits)]
    arrival = [1, 0] + list(range(2, len(candidates)))
    far_count = devices // GROUP
    near = [me - me % GROUP + (me + step) % GROUP for step in range(1, GROUP)]
    far = [(me + step * GROUP) % devices for step in range(1, far_count)]

    sources = [nodes_in, send_in, stiffness_in, region_in, mass_in, third_in, right_in, first_in, second_in]
    places = [nodes, send_nodes, stiffness, region, mass, third, right, first, second]
    loads = [
        pltpu.make_async_copy(source, place, in_sem.at[index])
        for index, (source, place) in enumerate(zip(sources, places))
    ]
    for load in loads:
        load.start()

    barrier = pltpu.get_barrier_semaphore()
    for other in candidates + near + far:
        pl.semaphore_signal(barrier, inc=1, device_id=(other,), device_id_type=MESH)

    node_table[...] = jnp.zeros_like(node_table)
    loads[0].wait()
    halves = [slice(half * LANES, (half + 1) * LANES) for half in range(elems // LANES)]
    for columns in halves:
        node_table[columns, :NPE] = nodes[:, columns].T
    table = node_table[...]
    own_count = pairs * LANES
    pair_of = lax.broadcasted_iota(jnp.int32, table.shape, 0) // 2
    key = jnp.where(
        table < own_count, table & (LANES - 1), LANES + ((table - run * pair_of) & (LANES - 1))
    )
    key_table[...] = jnp.where(
        lax.broadcasted_iota(jnp.int32, table.shape, 1) < NPE, key, 255
    ).astype(F32)
    stiff[...] = jnp.zeros_like(stiff)
    mass_term[...] = jnp.zeros_like(mass_term)
    for load in loads[1:6]:
        load.wait()
    for columns in halves:
        for axis in range(3):
            stiff[columns, axis * LANES : axis * LANES + NPE] = stiffness[axis, :, columns].T
        tag = region[:, columns]
        weight = jnp.where(tag == 0, density[0], jnp.where(tag == 1, density[1], density[2]))
        mass_term[columns, :NPE] = (mass[:, columns] * weight).T
    ghost[...] = jnp.zeros_like(ghost)

    diag_out = matmul(parts(stiff[...]), third[...])
    diag_term[...] = diag_out[:, :LANES] + diag_out[:, LANES:] + mass_term[...]

    def scatter_pair(pair, both, count):
        rows = jnp.concatenate([both, both - both.astype(BF16).astype(F32)], axis=0).astype(BF16)
        summed = matmul_nt(rows, hot[pair, :count])
        return summed[:NV] + summed[NV:]

    def gather_ghosts():
        sums = [jnp.zeros((NV, LANES), F32) for _ in range(peers)]
        lane = lax.broadcasted_iota(jnp.int32, (NV, LANES), 1)
        for pair in range(edge_pairs):
            base = pair * run
            begin = base % LANES
            row = ghost[pair]
            if begin:
                row = pltpu.roll(row, begin, 1)
            here, last = base // LANES, (base + run - 1) // LANES
            if here == last:
                sums[here] = sums[here] + row
            else:
                sums[here] = sums[here] + jnp.where(lane >= begin, row, 0.0)
                sums[last] = sums[last] + jnp.where(lane < begin, row, 0.0)
        return sums

    def remote(phase, j):
        return pltpu.make_async_remote_copy(
            src_ref=outgoing.at[phase, j],
            dst_ref=incoming[phase].at[arrival[j]],
            send_sem=send_sem.at[phase, j],
            recv_sem=recv_sem.at[phase, arrival[j]],
            device_id=(candidates[j],),
            device_id_type=MESH,
        )

    def slot_of(j):
        slot = jnp.int32(0)
        for p in range(peers):
            slot = jnp.where(peer_rank[0, p] == candidates[j], p, slot)
        return slot

    def candidate_of(p):
        found = jnp.int32(0)
        for j in range(len(candidates)):
            found = jnp.where(peer_rank[0, p] == candidates[j], j, found)
        return found

    slots_of = [slot_of(j) for j in range(len(candidates))]
    candidates_of = [candidate_of(p) for p in range(peers)]

    def send(phase, slot_values):
        for p in range(peers):
            compact[phase, p] = slot_values[p]
        for j in range(len(candidates)):
            outgoing[phase, j] = compact[phase, slots_of[j]]
            remote(phase, j).start()

    def receive(phase):
        for j in range(len(candidates)):
            remote(phase, j).wait_recv()
        return [incoming[phase][candidates_of[p]] for p in range(peers)]

    def add_returned(own, received):
        value = jnp.concatenate(received, axis=1)
        high = value.astype(BF16).astype(F32)
        low = jnp.concatenate([value - high] * 2, axis=0).astype(BF16)
        high = jnp.concatenate([high] * 2, axis=0).astype(BF16)
        window = jnp.broadcast_to((send_row // LANES).astype(F32), (2 * NV, live)).astype(BF16)
        second_row = lax.broadcasted_iota(jnp.int32, (2 * NV, live), 0) // NV
        none = jnp.zeros((2 * NV, live), BF16)

        def body(block, carry):
            high_rows, low_rows = [], []
            for i in range(WIDE // 2):
                number = (second_row + (block * WIDE + 2 * i)).astype(F32).astype(BF16)
                found = window == number
                high_rows.append(jnp.where(found, high, none))
                low_rows.append(jnp.where(found, low, none))
            at = pl.ds(pl.multiple_of(block * WIDE * NV, WIDE * NV), WIDE * NV)
            summed = matmul(jnp.concatenate(high_rows + low_rows, axis=0), back_hot[...])
            own[at, :] = own[at, :] + (summed[: WIDE * NV] + summed[WIDE * NV :])
            return carry

        lax.fori_loop(0, pairs // WIDE, body, 0)

    def pick_shared(load):
        def body(block, total):
            spread = matmul(parts(load(block)), lane_hot[...])
            for i in range(WIDE):
                total = total + jnp.where(
                    send_window == block * WIDE + i, spread[i * NV : (i + 1) * NV], 0.0
                )
            return total

        return lax.fori_loop(0, pairs // WIDE, body, jnp.zeros((NV, live), F32))

    def owned_rows(own):
        def load(block):
            return own[pl.ds(pl.multiple_of(block * WIDE * NV, WIDE * NV), WIDE * NV), :]

        return load

    def right_rows(block):
        base = block * WIDE * LANES
        return jnp.concatenate(
            [
                right[:, pl.ds(pl.multiple_of(base + i * LANES, LANES), LANES)]
                for i in range(WIDE)
            ],
            axis=0,
        )

    def pick_diagonal():
        spread = matmul(parts(diag_rows[...]), lane_hot[...])
        number = lax.broadcasted_iota(jnp.int32, (pairs, live), 0)
        found = jnp.where(number == send_row // LANES, spread, 0.0)
        return jnp.broadcast_to(jnp.sum(found, axis=0, keepdims=True), (NV, live))

    def add_shared(shared, received):
        value = jnp.concatenate(received, axis=1)
        rows = jnp.concatenate([value, value - value.astype(BF16).astype(F32)], axis=0).astype(BF16)
        summed = matmul(rows, same_hot[...])
        return shared + (summed[:NV] + summed[NV:])

    def slots(value):
        return [value[:, p * LANES : (p + 1) * LANES] for p in range(peers)]

    def build_and_scatter(edge):
        count = KEYS if edge else LANES
        row_of = lax.broadcasted_iota(jnp.int32, (16, 2 * LANES), 0)
        one, none = jnp.ones((16, 2 * LANES), BF16), jnp.zeros((16, 2 * LANES), BF16)

        def body(index, carry):
            pair = index if edge else index + edge_pairs
            both = pl.ds(2 * pair, 1), pl.ds(2 * pair + 1, 1)
            keys = jnp.concatenate([key_table[both[0], :], key_table[both[1], :]], axis=1)
            keys = jnp.broadcast_to(keys, (16, 2 * LANES)).astype(BF16)
            for tile in range(count // 16):
                number = (row_of + 16 * tile).astype(F32).astype(BF16)
                hot[pair, 16 * tile : 16 * tile + 16] = jnp.where(keys == number, one, none)
            term = jnp.concatenate([diag_term[both[0], :], diag_term[both[1], :]], axis=1)
            summed = scatter_pair(pair, jnp.broadcast_to(term, (NV, 2 * LANES)), count)
            at = pl.ds(pl.multiple_of(pair * NV, NV), NV)
            diagonal[at, :] = summed[:, :LANES]
            diag_rows[pl.ds(pair, 1), :] = summed[:1, :LANES]
            if edge:
                ghost[pair, :, : KEYS - LANES] = summed[:, LANES:]
            return carry

        lax.fori_loop(0, edge_pairs, body, 0, unroll=4)

    def apply_blocks(source, target, begin_block, end_block, total):
        edge = begin_block < edge_pairs // BLOCK

        def body(block, total):
            gathered = []
            for i in range(BLOCK):
                pair = block * BLOCK + i
                own = source[pl.ds(pl.multiple_of(pair * NV, NV), NV), :]
                if edge:
                    base = pair * run
                    lane = lax.broadcasted_iota(jnp.int32, (NV, LANES), 1)
                    begin = base % LANES
                    received = jnp.where(
                        lane >= begin, ordered[base // LANES], ordered[(base + run - 1) // LANES]
                    )
                for side in range(2):
                    node = jnp.broadcast_to(node_table[pl.ds(2 * pair + side, 1), :], (NV, LANES))
                    lanes = node & (LANES - 1)
                    picked = jnp.take_along_axis(own, lanes, axis=1, mode="promise_in_bounds")
                    if edge:
                        remote_value = jnp.take_along_axis(
                            received, lanes, axis=1, mode="promise_in_bounds"
                        )
                        picked = jnp.where(node < own_count, picked, remote_value)
                    gathered.append(picked)
            value = jnp.concatenate(gathered, axis=0)
            grad = matmul(parts(value), first[...])
            flux = grad[:, : 3 * LANES] + grad[:, 3 * LANES :]
            scaled = []
            masses = []
            for i in range(2 * BLOCK):
                at = pl.ds(block * 2 * BLOCK + i, 1)
                scaled.append(flux[i * NV : (i + 1) * NV] * stiff[at, :])
                masses.append(jnp.broadcast_to(mass_term[at, :], (NV, LANES)))
            back = matmul(parts(jnp.concatenate(scaled, axis=0)), second[...])
            result = back[:, :LANES] + back[:, LANES:] + jnp.concatenate(masses, axis=0) * value
            product = value * result
            for i in range(2 * BLOCK):
                total = total + product[i * NV : (i + 1) * NV]
            for i in range(BLOCK):
                pair = block * BLOCK + i
                low = 2 * i * NV
                both = jnp.concatenate(
                    [result[low : low + NV], result[low + NV : low + 2 * NV]], axis=1
                )
                summed = scatter_pair(pair, both, KEYS if edge else LANES)
                target[pl.ds(pl.multiple_of(pair * NV, NV), NV), :] = summed[:, :LANES]
                if edge:
                    ghost[pair, :, : KEYS - LANES] = summed[:, LANES:]
            return total

        return lax.fori_loop(begin_block, end_block, body, total)

    def over_pairs(step, total):
        def body(pair, total):
            return step(pair, pl.ds(pl.multiple_of(pair * NV, NV), NV), total)

        return lax.fori_loop(0, pairs, body, total, unroll=8)

    zero = jnp.zeros((NV, LANES), F32)
    build_and_scatter(True)
    pl.semaphore_wait(barrier, len(candidates) + len(near) + len(far))
    send(0, gather_ghosts())

    send_row = jnp.concatenate([send_nodes[p] for p in range(peers)], axis=1)
    send_window = jnp.broadcast_to(send_row // LANES, (NV, live))
    lane_number = lax.broadcasted_iota(jnp.int32, (LANES, live), 0)
    picks = (lane_number == (send_row & (LANES - 1))).astype(F32).astype(BF16)
    lane_hot[:LANES] = picks
    lane_hot[LANES:] = picks
    lane_number = lax.broadcasted_iota(jnp.int32, (LANES, LANES), 1)
    for p in range(peers):
        column = jnp.broadcast_to(send_nodes[p], (LANES, LANES)).T
        rows = slice(p * LANES, (p + 1) * LANES)
        back_hot[rows] = (lane_number == (column & (LANES - 1))).astype(F32).astype(BF16)
        for other in range(peers):
            same_hot[rows, other * LANES : (other + 1) * LANES] = (
                (column == send_nodes[other]).astype(F32).astype(BF16)
            )
    build_and_scatter(False)
    for load in loads[6:]:
        load.wait()
    right_shared = pick_shared(right_rows)
    diag_shared = pick_diagonal()
    received = receive(0)
    diag_shared = add_shared(diag_shared, received)
    send(1, slots(right_shared / diag_shared))
    add_returned(diagonal, received)

    def begin(pair, at, total):
        value = right[:, pl.ds(pl.multiple_of(pair * LANES, LANES), LANES)]
        scaled = value / diagonal[at, :]
        z_own[at, :] = scaled
        return total + value * scaled

    sum_rz = over_pairs(begin, zero)
    blocks = pairs // BLOCK
    edge_blocks = edge_pairs // BLOCK
    early = edge_blocks + (blocks - edge_blocks) // 2

    def order(phase):
        for p, value in enumerate(receive(phase)):
            ordered[p] = value

    sum_zw = apply_blocks(z_own, w_own, edge_blocks, early, zero)
    order(1)
    sum_zw = apply_blocks(z_own, w_own, 0, edge_blocks, sum_zw)
    send(2, gather_ghosts())
    sum_zw = apply_blocks(z_own, w_own, early, blocks, sum_zw)
    image_shared = pick_shared(owned_rows(w_own))
    received = receive(2)
    image_shared = add_shared(image_shared, received)
    send(3, slots(image_shared / diag_shared))
    add_returned(w_own, received)

    def middle(pair, at, total):
        value = w_own[at, :]
        scaled = value / diagonal[at, :]
        q_own[at, :] = scaled
        return total + value * scaled

    sum_wq = over_pairs(middle, zero)
    sum_qp = apply_blocks(q_own, p_own, edge_blocks, blocks, zero)
    order(3)
    sum_qp = apply_blocks(q_own, p_own, 0, edge_blocks, sum_qp)
    send(4, gather_ghosts())

    lane = lax.broadcasted_iota(jnp.int32, (NV, LANES), 1)
    quarter = LANES // 4
    packed = zero
    for place, total in enumerate((sum_rz, sum_zw, sum_wq, sum_qp)):
        total = total + pltpu.roll(total, LANES // 2, 1)
        total = total + pltpu.roll(total, quarter, 1)
        packed = jnp.where(lane // quarter == place, total, packed)

    def near_copy(step):
        return pltpu.make_async_remote_copy(
            src_ref=partial.at[0],
            dst_ref=near_in.at[step],
            send_sem=near_send.at[step],
            recv_sem=near_recv.at[step],
            device_id=(near[step],),
            device_id_type=MESH,
        )

    def far_copy(step):
        return pltpu.make_async_remote_copy(
            src_ref=partial.at[1],
            dst_ref=far_in.at[step],
            send_sem=far_send.at[step],
            recv_sem=far_recv.at[step],
            device_id=(far[step],),
            device_id_type=MESH,
        )

    partial[0] = packed
    for step in range(len(near)):
        near_copy(step).start()
    for step in range(len(near)):
        near_copy(step).wait_recv()
        packed = packed + near_in[step]
    partial[1] = packed
    for step in range(len(far)):
        far_copy(step).start()
    add_returned(p_own, receive(4))
    for step in range(len(far)):
        far_copy(step).wait_recv()
        packed = packed + far_in[step]
    rz, zw, wq, qp = [
        jnp.sum(jnp.where(lane // quarter == place, packed, 0.0), axis=1, keepdims=True)
        for place in range(4)
    ]
    alpha = rz / zw
    new = rz - 2.0 * alpha * zw + alpha * alpha * wq
    ratio = 1.0 + new / rz
    second_alpha = new / (
        ratio * ratio * zw - 2.0 * alpha * ratio * wq + alpha * alpha * qp
    )
    outer = jnp.broadcast_to(alpha + second_alpha * ratio, (NV, LANES))
    inner = jnp.broadcast_to(alpha * second_alpha, (NV, LANES))

    def finish(pair, at, total):
        out = pl.ds(pl.multiple_of(pair * LANES, LANES), LANES)
        solution_out[:, out] = outer * z_own[at, :] - inner * q_own[at, :]
        residual_out[:, out] = right[:, out] - outer * w_own[at, :] + inner * p_own[at, :]
        return total

    over_pairs(finish, zero)
    for phase in range(5):
        for j in range(len(candidates)):
            remote(phase, j).wait_send()
    for step in range(len(near)):
        near_copy(step).wait_send()
    for step in range(len(far)):
        far_copy(step).wait_send()


def on_device(devices, right, stiffness, mass, region, density, elem_nodes, peer_rank, send_nodes):
    first, second, third = (jnp.asarray(matrix) for matrix in operator_matrices())
    own_count = right.shape[1]
    elems = elem_nodes.shape[1]
    pairs = elems // 2
    peers = send_nodes.shape[1]
    live = peers * LANES
    bits = devices.bit_length() - 1
    ways = bits + 1
    near_count, far_count = GROUP - 1, devices // GROUP - 1
    vmem = pl.BlockSpec(memory_space=pltpu.VMEM)
    smem = pl.BlockSpec(memory_space=pltpu.SMEM)
    hbm = pl.BlockSpec(memory_space=pltpu.HBM)
    owned = pltpu.VMEM((pairs * NV, LANES), F32)
    dma = pltpu.SemaphoreType.DMA
    return pl.pallas_call(
        functools.partial(kernel, devices),
        out_shape=(
            jax.ShapeDtypeStruct((NV, own_count), F32),
            jax.ShapeDtypeStruct((NV, own_count), F32),
        ),
        in_specs=[smem, smem] + [hbm] * 9,
        out_specs=(vmem, vmem),
        scratch_shapes=[
            pltpu.VMEM((NV, own_count), F32),
            pltpu.VMEM(stiffness.shape, F32),
            pltpu.VMEM(mass.shape, F32),
            pltpu.VMEM((1, elems), jnp.int32),
            pltpu.VMEM(elem_nodes.shape, jnp.int32),
            pltpu.VMEM((peers, 1, LANES), jnp.int32),
            pltpu.VMEM(first.shape, BF16),
            pltpu.VMEM(second.shape, BF16),
            pltpu.VMEM(third.shape, BF16),
            dma((9,)),
            pltpu.VMEM((elems, 3 * LANES), F32),
            pltpu.VMEM((elems, LANES), F32),
            pltpu.VMEM((elems, LANES), jnp.int32),
            pltpu.VMEM((elems, LANES), F32),
            pltpu.VMEM((pairs, KEYS, 2 * LANES), BF16),
            pltpu.VMEM((elems, LANES), F32),
            owned,
            owned,
            owned,
            owned,
            owned,
            pltpu.VMEM((2 * LANES, live), BF16),
            pltpu.VMEM((live, LANES), BF16),
            pltpu.VMEM((live, live), BF16),
            pltpu.VMEM((pairs, LANES), F32),
            pltpu.VMEM((pairs // 2, NV, LANES), F32),
            pltpu.VMEM((5, peers, NV, LANES), F32),
            pltpu.VMEM((5, ways, NV, LANES), F32),
            pltpu.VMEM((ways, NV, LANES), F32),
            pltpu.VMEM((ways, NV, LANES), F32),
            pltpu.VMEM((ways, NV, LANES), F32),
            pltpu.VMEM((ways, NV, LANES), F32),
            pltpu.VMEM((ways, NV, LANES), F32),
            pltpu.VMEM((peers, NV, LANES), F32),
            dma((5, ways)),
            dma((5, ways)),
            pltpu.VMEM((2, NV, LANES), F32),
            pltpu.VMEM((near_count, NV, LANES), F32),
            pltpu.VMEM((far_count, NV, LANES), F32),
            dma((near_count,)),
            dma((near_count,)),
            dma((far_count,)),
            dma((far_count,)),
        ],
        compiler_params=pltpu.CompilerParams(
            collective_id=0, has_side_effects=True, vmem_limit_bytes=60 * 1024 * 1024
        ),
    )(
        density,
        peer_rank,
        right,
        stiffness,
        mass,
        region.reshape(1, elems),
        elem_nodes,
        jnp.transpose(send_nodes, (1, 0, 2)),
        first,
        second,
        third,
    )


def solution(mesh):
    devices = mesh.shape["dom"]
    placed = (
        P(None, "dom"),
        P(None, None, "dom"),
        P(None, "dom"),
        P("dom"),
        P(),
        P(None, "dom"),
        P("dom", None),
        P("dom", None, None),
    )
    return jax.shard_map(
        functools.partial(on_device, devices),
        mesh=mesh,
        in_specs=placed,
        out_specs=(P(None, "dom"), P(None, "dom")),
        check_vma=False,
    )
```

```python
import functools

import jax
import jax.numpy as jnp
import numpy as np
from jax import lax
from jax.experimental import pallas as pl
from jax.experimental.pallas import tpu as pltpu
from jax.sharding import PartitionSpec as P

MESH = pl.DeviceIdType.MESH
F32 = jnp.float32
BF16 = jnp.bfloat16
NV = 8
NPE = 125
LANES = 128
GROUP = 8
KEYS = 144
BLOCK = 32
WIDE = 32


def gll_matrix():
    points = np.array([-1.0, -np.sqrt(3.0 / 7.0), 0.0, np.sqrt(3.0 / 7.0), 1.0])
    weights = np.array(
        [
            1.0 / np.prod([points[column] - points[other] for other in range(5) if other != column])
            for column in range(5)
        ]
    )
    matrix = np.zeros((5, 5))
    for row_index in range(5):
        for column in range(5):
            if row_index != column:
                matrix[row_index, column] = (
                    weights[column] / weights[row_index] / (points[row_index] - points[column])
                )
        matrix[row_index, row_index] = -np.sum(matrix[row_index])
    return matrix


def split_numpy(matrix):
    single = matrix.astype(np.float32)
    high = single.astype(jnp.bfloat16)
    low = (single - high.astype(np.float32)).astype(jnp.bfloat16)
    return high, low


SCALED = np.array(
    [
        [-6.09375, 6.8125, -4.875, 1.421875, -0.609375],
        [-1.703125, 0.0, 3.59375, -0.8671875, 0.35546875],
        [0.609375, -1.796875, 0.0, 1.796875, -0.609375],
        [-0.35546875, 0.8671875, -3.59375, 0.0, 1.703125],
        [0.609375, -1.421875, 4.875, -6.8125, 6.09375],
    ]
)


def scales():
    matrix = gll_matrix()
    equations, logs = [], []
    for a in range(5):
        for i in range(5):
            if a != i or a in (0, 4):
                equation = np.zeros(10)
                equation[a] = equation[5 + i] = abs(matrix[a, i])
                equations.append(equation)
                logs.append(abs(matrix[a, i]) * np.log(SCALED[a, i] / matrix[a, i]))
    fitted = np.linalg.lstsq(np.array(equations), np.array(logs), rcond=None)[0]
    return np.exp(fitted[:5]), np.exp(fitted[5:])


def operator_matrices():
    eye = np.eye(5)

    def along(small):
        full = np.zeros((3, LANES, LANES))
        full[0, :NPE, :NPE] = np.kron(np.kron(small, eye), eye)
        full[1, :NPE, :NPE] = np.kron(np.kron(eye, small), eye)
        full[2, :NPE, :NPE] = np.kron(np.kron(eye, eye), small)
        return full

    first = np.concatenate([full.T for full in along(SCALED)], axis=1).astype(jnp.bfloat16)
    first = np.concatenate([first, first], axis=0)
    second = np.concatenate(list(along(SCALED)), axis=0).astype(jnp.bfloat16)
    second = np.concatenate([second, second], axis=0)
    square = np.concatenate(list(along(SCALED * SCALED)), axis=0)
    third = np.concatenate(split_numpy(square), axis=1)
    third = np.concatenate([third, third], axis=0)
    row, column = scales()
    of_flux = np.zeros((1, 3 * LANES), np.float32)
    for axis in range(3):
        factors = [column, column, column]
        factors[axis] = 1.0 / row
        product = np.kron(np.kron(factors[0], factors[1]), factors[2])
        of_flux[0, axis * LANES : axis * LANES + NPE] = product * product
    of_value = np.zeros((1, LANES), np.float32)
    of_value[0, :NPE] = 1.0 / np.kron(np.kron(column, column), column)
    return first, second, third, of_flux, of_value


def split(value):
    high = value.astype(BF16)
    return high, (value - high.astype(F32)).astype(BF16)


def parts(value):
    return jnp.concatenate(split(value), axis=1)


def matmul(left, right):
    return lax.dot_general(left, right, (((1,), (0,)), ((), ())), preferred_element_type=F32)


def matmul_nt(left, right):
    return lax.dot_general(left, right, (((1,), (1,)), ((), ())), preferred_element_type=F32)


def flipped(rank, bit):
    return rank + bit - 2 * bit * ((rank // bit) % 2)


def kernel(
    devices,
    density,
    peer_rank,
    right_in,
    stiffness_in,
    mass_in,
    region_in,
    nodes_in,
    send_in,
    first_in,
    second_in,
    third_in,
    of_flux,
    of_value,
    solution_out,
    residual_out,
    right,
    stiffness,
    mass,
    region,
    nodes,
    send_nodes,
    first,
    second,
    third,
    in_sem,
    stiff,
    mass_term,
    node_table,
    key_table,
    hot,
    ghost_hot,
    results,
    diag_term,
    diagonal,
    z_own,
    w_own,
    q_own,
    p_own,
    lane_hot,
    back_hot,
    same_hot,
    diag_rows,
    ghost,
    compact,
    outgoing,
    incoming_0,
    incoming_1,
    incoming_2,
    incoming_3,
    incoming_4,
    ordered,
    send_sem,
    recv_sem,
    partial,
    near_in,
    far_in,
    near_send,
    near_recv,
    far_send,
    far_recv,
):
    me = lax.axis_index("dom")

    def tile(pair):
        return slice(None), pl.ds(pl.multiple_of(pair * LANES, LANES), LANES)

    incoming = [incoming_0, incoming_1, incoming_2, incoming_3, incoming_4]
    elems = nodes.shape[1]
    pairs = elems // 2
    edge_pairs = pairs // 2
    peers = send_nodes.shape[0]
    live = peers * LANES
    run = live // edge_pairs
    bits = devices.bit_length() - 1
    candidates = [(me + 1) % devices, (me + devices - 1) % devices]
    candidates += [flipped(me, 2**k) for k in range(1, bits)]
    arrival = [1, 0] + list(range(2, len(candidates)))
    far_count = devices // GROUP
    near = [me - me % GROUP + (me + step) % GROUP for step in range(1, GROUP)]
    far = [(me + step * GROUP) % devices for step in range(1, far_count)]

    sources = [nodes_in, send_in, stiffness_in, region_in, mass_in, third_in, right_in, first_in, second_in]
    places = [nodes, send_nodes, stiffness, region, mass, third, right, first, second]
    loads = [
        pltpu.make_async_copy(source, place, in_sem.at[index])
        for index, (source, place) in enumerate(zip(sources, places))
    ]
    for load in loads:
        load.start()

    barrier = pltpu.get_barrier_semaphore()
    for other in candidates + near + far:
        pl.semaphore_signal(barrier, inc=1, device_id=(other,), device_id_type=MESH)

    own_count = pairs * LANES
    value_scale = of_value[...]

    def tables(half):
        columns = slice(half * LANES, (half + 1) * LANES)
        node_table[columns] = jnp.zeros((LANES, LANES), jnp.int32)
        node_table[columns, :NPE] = nodes[:, columns].T
        table = node_table[columns]
        pair_of = half * (LANES // 2) + lax.broadcasted_iota(jnp.int32, table.shape, 0) // 2
        key = jnp.where(
            table < own_count, table & (LANES - 1), LANES + ((table - run * pair_of) & (LANES - 1))
        )
        key_table[columns] = jnp.where(
            lax.broadcasted_iota(jnp.int32, table.shape, 1) < NPE, key, 255
        ).astype(F32)
        stiff[columns] = jnp.zeros((LANES, 3 * LANES), F32)
        mass_term[columns] = jnp.zeros((LANES, LANES), F32)
        for axis in range(3):
            at = slice(axis * LANES, axis * LANES + NPE)
            stiff[columns, at] = stiffness[axis, :, columns].T * of_flux[:, at]
        tag = region[:, columns]
        weight = jnp.where(tag == 0, density[0], jnp.where(tag == 1, density[1], density[2]))
        mass_term[columns, :NPE] = (mass[:, columns] * weight).T
        diag_out = matmul(parts(stiff[columns]), third[...])
        diag_term[columns] = (diag_out[:, :LANES] + diag_out[:, LANES:]) * (
            value_scale * value_scale
        ) + mass_term[columns]

    ghost[...] = jnp.zeros_like(ghost)
    for load in loads[:6]:
        load.wait()
    tables(0)

    def scatter_rows(both, where):
        rows = jnp.concatenate([both, both - both.astype(BF16).astype(F32)], axis=0).astype(BF16)
        summed = matmul_nt(rows, where)
        return summed[:NV] + summed[NV:]

    def scatter_pair(pair, both):
        return scatter_rows(both, hot[pair])

    def gather_ghosts():
        sums = [jnp.zeros((NV, LANES), F32) for _ in range(peers)]
        lane = lax.broadcasted_iota(jnp.int32, (NV, LANES), 1)
        for pair in range(edge_pairs):
            base = pair * run
            begin = base % LANES
            row = ghost[pair]
            if begin:
                row = pltpu.roll(row, begin, 1)
            here, last = base // LANES, (base + run - 1) // LANES
            if here == last:
                sums[here] = sums[here] + row
            else:
                sums[here] = sums[here] + jnp.where(lane >= begin, row, 0.0)
                sums[last] = sums[last] + jnp.where(lane < begin, row, 0.0)
        return sums

    def remote(phase, j):
        return pltpu.make_async_remote_copy(
            src_ref=outgoing.at[phase, j],
            dst_ref=incoming[phase].at[arrival[j]],
            send_sem=send_sem.at[phase, j],
            recv_sem=recv_sem.at[phase, arrival[j]],
            device_id=(candidates[j],),
            device_id_type=MESH,
        )

    def slot_of(j):
        slot = jnp.int32(0)
        for p in range(peers):
            slot = jnp.where(peer_rank[0, p] == candidates[j], p, slot)
        return slot

    def candidate_of(p):
        found = jnp.int32(0)
        for j in range(len(candidates)):
            found = jnp.where(peer_rank[0, p] == candidates[j], j, found)
        return found

    slots_of = [slot_of(j) for j in range(len(candidates))]
    candidates_of = [candidate_of(p) for p in range(peers)]

    def send(phase, slot_values):
        for p in range(peers):
            compact[phase, p] = slot_values[p]
        for j in range(len(candidates)):
            outgoing[phase, j] = compact[phase, slots_of[j]]
            remote(phase, j).start()

    def receive(phase):
        for j in range(len(candidates)):
            remote(phase, j).wait_recv()
        return [incoming[phase][candidates_of[p]] for p in range(peers)]

    def add_returned(own, received):
        value = jnp.concatenate(received, axis=1)
        high = value.astype(BF16).astype(F32)
        low = jnp.concatenate([value - high] * 2, axis=0).astype(BF16)
        high = jnp.concatenate([high] * 2, axis=0).astype(BF16)
        window = jnp.broadcast_to((send_row // LANES).astype(F32), (2 * NV, live)).astype(BF16)
        second_row = lax.broadcasted_iota(jnp.int32, (2 * NV, live), 0) // NV
        none = jnp.zeros((2 * NV, live), BF16)

        def body(block, carry):
            high_rows, low_rows = [], []
            for i in range(WIDE // 2):
                number = (second_row + (block * WIDE + 2 * i)).astype(F32).astype(BF16)
                found = window == number
                high_rows.append(jnp.where(found, high, none))
                low_rows.append(jnp.where(found, low, none))
            summed = matmul(jnp.concatenate(high_rows + low_rows, axis=0), back_hot[...])
            summed = summed[: WIDE * NV] + summed[WIDE * NV :]
            for i in range(WIDE):
                at = tile(block * WIDE + i)
                own[at] = own[at] + summed[i * NV : (i + 1) * NV]
            return carry

        lax.fori_loop(0, pairs // WIDE, body, 0)

    def pick_shared(own):
        def body(block, total):
            rows = jnp.concatenate([own[tile(block * WIDE + i)] for i in range(WIDE)], axis=0)
            spread = matmul(parts(rows), lane_hot[...])
            for i in range(WIDE):
                total = total + jnp.where(
                    send_window == block * WIDE + i, spread[i * NV : (i + 1) * NV], 0.0
                )
            return total

        return lax.fori_loop(0, pairs // WIDE, body, jnp.zeros((NV, live), F32))

    def pick_diagonal():
        spread = matmul(parts(diag_rows[...]), lane_hot[...])
        number = lax.broadcasted_iota(jnp.int32, (pairs, live), 0)
        found = jnp.where(number == send_row // LANES, spread, 0.0)
        return jnp.broadcast_to(jnp.sum(found, axis=0, keepdims=True), (NV, live))

    def add_shared(shared, received):
        value = jnp.concatenate(received, axis=1)
        rows = jnp.concatenate([value, value - value.astype(BF16).astype(F32)], axis=0).astype(BF16)
        summed = matmul(rows, same_hot[...])
        return shared + (summed[:NV] + summed[NV:])

    def slots(value):
        return [value[:, p * LANES : (p + 1) * LANES] for p in range(peers)]

    row_of = lax.broadcasted_iota(jnp.int32, (16, 2 * LANES), 0)
    one, none = jnp.ones((16, 2 * LANES), BF16), jnp.zeros((16, 2 * LANES), BF16)

    def keys_of(pair):
        both = pl.ds(2 * pair, 1), pl.ds(2 * pair + 1, 1)
        keys = jnp.concatenate([key_table[both[0], :], key_table[both[1], :]], axis=1)
        return jnp.broadcast_to(keys, (16, 2 * LANES)).astype(BF16)

    def diag_of(pair):
        both = pl.ds(2 * pair, 1), pl.ds(2 * pair + 1, 1)
        term = jnp.concatenate([diag_term[both[0], :], diag_term[both[1], :]], axis=1)
        return jnp.broadcast_to(term, (NV, 2 * LANES))

    def strip(keys, begin):
        number = (row_of + begin).astype(F32).astype(BF16)
        return jnp.where(keys == number, one, none)

    def build_ghosts():
        def body(pair, carry):
            where = strip(keys_of(pair), LANES)
            ghost_hot[pair] = where
            ghost[pair, :, : KEYS - LANES] = scatter_rows(diag_of(pair), where)
            return carry

        lax.fori_loop(0, edge_pairs, body, 0, unroll=8)

    def build_owned():
        def body(pair, carry):
            keys = keys_of(pair)
            for begin in range(0, LANES, 16):
                hot[pair, begin : begin + 16] = strip(keys, begin)
            summed = scatter_pair(pair, diag_of(pair))
            diagonal[tile(pair)] = summed
            diag_rows[pl.ds(pair, 1), :] = summed[:1]
            return carry

        lax.fori_loop(0, pairs, body, 0, unroll=4)

    def apply_blocks(source, target, begin_block, end_block, total):
        edge = begin_block < edge_pairs // BLOCK

        def body(block, total):
            gathered = []
            for i in range(BLOCK):
                pair = block * BLOCK + i
                own = source[tile(pair)]
                if edge:
                    base = pair * run
                    lane = lax.broadcasted_iota(jnp.int32, (NV, LANES), 1)
                    begin = base % LANES
                    received = jnp.where(
                        lane >= begin, ordered[base // LANES], ordered[(base + run - 1) // LANES]
                    )
                for side in range(2):
                    node = jnp.broadcast_to(node_table[pl.ds(2 * pair + side, 1), :], (NV, LANES))
                    lanes = node & (LANES - 1)
                    picked = jnp.take_along_axis(own, lanes, axis=1, mode="promise_in_bounds")
                    if edge:
                        remote_value = jnp.take_along_axis(
                            received, lanes, axis=1, mode="promise_in_bounds"
                        )
                        picked = jnp.where(node < own_count, picked, remote_value)
                    gathered.append(picked)
            value = jnp.concatenate(gathered, axis=0)
            flux = matmul(parts(value * value_scale), first[...])
            scaled = []
            masses = []
            for i in range(2 * BLOCK):
                at = pl.ds(block * 2 * BLOCK + i, 1)
                scaled.append(flux[i * NV : (i + 1) * NV] * stiff[at, :])
                masses.append(jnp.broadcast_to(mass_term[at, :], (NV, LANES)))
            back = matmul(parts(jnp.concatenate(scaled, axis=0)), second[...])
            result = back * value_scale + jnp.concatenate(masses, axis=0) * value
            product = value * result
            for i in range(2 * BLOCK):
                total = total + product[i * NV : (i + 1) * NV]
            for i in range(BLOCK):
                pair = block * BLOCK + i
                low = 2 * i * NV
                both = jnp.concatenate(
                    [result[low : low + NV], result[low + NV : low + 2 * NV]], axis=1
                )
                if edge:
                    results[pair] = both
                    ghost[pair, :, : KEYS - LANES] = scatter_rows(both, ghost_hot[pair])
                else:
                    target[tile(pair)] = scatter_pair(pair, both)
            return total

        return lax.fori_loop(begin_block, end_block, body, total)

    def place_edge(target):
        def body(pair, carry):
            target[tile(pair)] = scatter_pair(pair, results[pair])
            return carry

        lax.fori_loop(0, edge_pairs, body, 0, unroll=8)

    def over_pairs(step, total):
        def body(pair, total):
            return step(tile(pair), total)

        return lax.fori_loop(0, pairs, body, total, unroll=8)

    zero = jnp.zeros((NV, LANES), F32)
    build_ghosts()
    pl.semaphore_wait(barrier, len(candidates) + len(near) + len(far))
    send(0, gather_ghosts())

    send_row = jnp.concatenate([send_nodes[p] for p in range(peers)], axis=1)
    send_window = jnp.broadcast_to(send_row // LANES, (NV, live))
    lane_number = lax.broadcasted_iota(jnp.int32, (LANES, live), 0)
    picks = (lane_number == (send_row & (LANES - 1))).astype(F32).astype(BF16)
    lane_hot[:LANES] = picks
    lane_hot[LANES:] = picks
    lane_number = lax.broadcasted_iota(jnp.int32, (LANES, LANES), 1)
    for p in range(peers):
        column = jnp.broadcast_to(send_nodes[p], (LANES, LANES)).T
        rows = slice(p * LANES, (p + 1) * LANES)
        back_hot[rows] = (lane_number == (column & (LANES - 1))).astype(F32).astype(BF16)
        for other in range(peers):
            same_hot[rows, other * LANES : (other + 1) * LANES] = (
                (column == send_nodes[other]).astype(F32).astype(BF16)
            )
    tables(1)
    build_owned()
    for load in loads[6:]:
        load.wait()
    right_shared = pick_shared(right)
    diag_shared = pick_diagonal()
    received = receive(0)
    diag_shared = add_shared(diag_shared, received)
    send(1, slots(right_shared / diag_shared))
    add_returned(diagonal, received)

    def begin(at, total):
        value = right[at]
        scaled = value / diagonal[at]
        z_own[at] = scaled
        return total + value * scaled

    sum_rz = over_pairs(begin, zero)
    blocks = pairs // BLOCK
    edge_blocks = edge_pairs // BLOCK
    early = edge_blocks + (blocks - edge_blocks) // 2

    def order(phase):
        for p, value in enumerate(receive(phase)):
            ordered[p] = value

    sum_zw = apply_blocks(z_own, w_own, edge_blocks, early, zero)
    order(1)
    sum_zw = apply_blocks(z_own, w_own, 0, edge_blocks, sum_zw)
    send(2, gather_ghosts())
    place_edge(w_own)
    sum_zw = apply_blocks(z_own, w_own, early, blocks, sum_zw)
    image_shared = pick_shared(w_own)
    received = receive(2)
    image_shared = add_shared(image_shared, received)
    send(3, slots(image_shared / diag_shared))
    add_returned(w_own, received)

    def middle(at, total):
        value = w_own[at]
        scaled = value / diagonal[at]
        q_own[at] = scaled
        return total + value * scaled

    sum_wq = over_pairs(middle, zero)
    sum_qp = apply_blocks(q_own, p_own, edge_blocks, blocks, zero)
    order(3)
    sum_qp = apply_blocks(q_own, p_own, 0, edge_blocks, sum_qp)
    send(4, gather_ghosts())

    lane = lax.broadcasted_iota(jnp.int32, (NV, LANES), 1)
    quarter = LANES // 4
    packed = zero
    for place, total in enumerate((sum_rz, sum_zw, sum_wq, sum_qp)):
        total = total + pltpu.roll(total, LANES // 2, 1)
        total = total + pltpu.roll(total, quarter, 1)
        packed = jnp.where(lane // quarter == place, total, packed)

    def near_copy(step):
        return pltpu.make_async_remote_copy(
            src_ref=partial.at[0],
            dst_ref=near_in.at[step],
            send_sem=near_send.at[step],
            recv_sem=near_recv.at[step],
            device_id=(near[step],),
            device_id_type=MESH,
        )

    def far_copy(step):
        return pltpu.make_async_remote_copy(
            src_ref=partial.at[1],
            dst_ref=far_in.at[step],
            send_sem=far_send.at[step],
            recv_sem=far_recv.at[step],
            device_id=(far[step],),
            device_id_type=MESH,
        )

    partial[0] = packed
    for step in range(len(near)):
        near_copy(step).start()
    place_edge(p_own)
    for step in range(len(near)):
        near_copy(step).wait_recv()
        packed = packed + near_in[step]
    partial[1] = packed
    for step in range(len(far)):
        far_copy(step).start()
    add_returned(p_own, receive(4))
    for step in range(len(far)):
        far_copy(step).wait_recv()
        packed = packed + far_in[step]
    rz, zw, wq, qp = [
        jnp.sum(jnp.where(lane // quarter == place, packed, 0.0), axis=1, keepdims=True)
        for place in range(4)
    ]
    alpha = rz / zw
    new = rz - 2.0 * alpha * zw + alpha * alpha * wq
    ratio = 1.0 + new / rz
    second_alpha = new / (
        ratio * ratio * zw - 2.0 * alpha * ratio * wq + alpha * alpha * qp
    )
    outer = jnp.broadcast_to(alpha + second_alpha * ratio, (NV, LANES))
    inner = jnp.broadcast_to(alpha * second_alpha, (NV, LANES))

    def finish(at, total):
        solution_out[at] = outer * z_own[at] - inner * q_own[at]
        residual_out[at] = right[at] - outer * w_own[at] + inner * p_own[at]
        return total

    over_pairs(finish, zero)
    for phase in range(5):
        for j in range(len(candidates)):
            remote(phase, j).wait_send()
    for step in range(len(near)):
        near_copy(step).wait_send()
    for step in range(len(far)):
        far_copy(step).wait_send()


def on_device(devices, right, stiffness, mass, region, density, elem_nodes, peer_rank, send_nodes):
    first, second, third, of_flux, of_value = (
        jnp.asarray(matrix) for matrix in operator_matrices()
    )
    own_count = right.shape[1]
    elems = elem_nodes.shape[1]
    pairs = elems // 2
    peers = send_nodes.shape[1]
    live = peers * LANES
    bits = devices.bit_length() - 1
    ways = bits + 1
    near_count, far_count = GROUP - 1, devices // GROUP - 1
    vmem = pl.BlockSpec(memory_space=pltpu.VMEM)
    smem = pl.BlockSpec(memory_space=pltpu.SMEM)
    hbm = pl.BlockSpec(memory_space=pltpu.HBM)
    owned = pltpu.VMEM((NV, own_count), F32)
    dma = pltpu.SemaphoreType.DMA
    return pl.pallas_call(
        functools.partial(kernel, devices),
        out_shape=(jax.ShapeDtypeStruct((NV, own_count), F32),) * 2,
        in_specs=[smem, smem] + [hbm] * 9 + [vmem] * 2,
        out_specs=(vmem, vmem),
        scratch_shapes=[
            pltpu.VMEM((NV, own_count), F32),
            pltpu.VMEM(stiffness.shape, F32),
            pltpu.VMEM(mass.shape, F32),
            pltpu.VMEM((1, elems), jnp.int32),
            pltpu.VMEM(elem_nodes.shape, jnp.int32),
            pltpu.VMEM((peers, 1, LANES), jnp.int32),
            pltpu.VMEM(first.shape, BF16),
            pltpu.VMEM(second.shape, BF16),
            pltpu.VMEM(third.shape, BF16),
            dma((9,)),
            pltpu.VMEM((elems, 3 * LANES), F32),
            pltpu.VMEM((elems, LANES), F32),
            pltpu.VMEM((elems, LANES), jnp.int32),
            pltpu.VMEM((elems, LANES), F32),
            pltpu.VMEM((pairs, LANES, 2 * LANES), BF16),
            pltpu.VMEM((pairs // 2, KEYS - LANES, 2 * LANES), BF16),
            pltpu.VMEM((pairs // 2, NV, 2 * LANES), F32),
            pltpu.VMEM((elems, LANES), F32),
            owned,
            owned,
            owned,
            owned,
            owned,
            pltpu.VMEM((2 * LANES, live), BF16),
            pltpu.VMEM((live, LANES), BF16),
            pltpu.VMEM((live, live), BF16),
            pltpu.VMEM((pairs, LANES), F32),
            pltpu.VMEM((pairs // 2, NV, LANES), F32),
            pltpu.VMEM((5, peers, NV, LANES), F32),
            pltpu.VMEM((5, ways, NV, LANES), F32),
            pltpu.VMEM((ways, NV, LANES), F32),
            pltpu.VMEM((ways, NV, LANES), F32),
            pltpu.VMEM((ways, NV, LANES), F32),
            pltpu.VMEM((ways, NV, LANES), F32),
            pltpu.VMEM((ways, NV, LANES), F32),
            pltpu.VMEM((peers, NV, LANES), F32),
            dma((5, ways)),
            dma((5, ways)),
            pltpu.VMEM((2, NV, LANES), F32),
            pltpu.VMEM((near_count, NV, LANES), F32),
            pltpu.VMEM((far_count, NV, LANES), F32),
            dma((near_count,)),
            dma((near_count,)),
            dma((far_count,)),
            dma((far_count,)),
        ],
        compiler_params=pltpu.CompilerParams(
            collective_id=0, has_side_effects=True, vmem_limit_bytes=60 * 1024 * 1024
        ),
    )(
        density,
        peer_rank,
        right,
        stiffness,
        mass,
        region.reshape(1, elems),
        elem_nodes,
        jnp.transpose(send_nodes, (1, 0, 2)),
        first,
        second,
        third,
        of_flux,
        of_value,
    )


def solution(mesh):
    devices = mesh.shape["dom"]
    placed = (
        P(None, "dom"),
        P(None, None, "dom"),
        P(None, "dom"),
        P("dom"),
        P(),
        P(None, "dom"),
        P("dom", None),
        P("dom", None, None),
    )
    return jax.shard_map(
        functools.partial(on_device, devices),
        mesh=mesh,
        in_specs=placed,
        out_specs=(P(None, "dom"), P(None, "dom")),
        check_vma=False,
    )
```

```python
import functools

import jax
import jax.numpy as jnp
import numpy as np
from jax import lax
from jax.experimental import pallas as pl
from jax.experimental.pallas import tpu as pltpu
from jax.sharding import PartitionSpec as P

MESH = pl.DeviceIdType.MESH
F32 = jnp.float32
BF16 = jnp.bfloat16
NV = 8
NPE = 125
LANES = 128
GROUP = 8
KEYS = 144
BLOCK = 32
WIDE = 32
PICK = 64


def gll_matrix():
    points = np.array([-1.0, -np.sqrt(3.0 / 7.0), 0.0, np.sqrt(3.0 / 7.0), 1.0])
    weights = np.array(
        [
            1.0 / np.prod([points[column] - points[other] for other in range(5) if other != column])
            for column in range(5)
        ]
    )
    matrix = np.zeros((5, 5))
    for row_index in range(5):
        for column in range(5):
            if row_index != column:
                matrix[row_index, column] = (
                    weights[column] / weights[row_index] / (points[row_index] - points[column])
                )
        matrix[row_index, row_index] = -np.sum(matrix[row_index])
    return matrix


def split_numpy(matrix):
    single = matrix.astype(np.float32)
    high = single.astype(jnp.bfloat16)
    low = (single - high.astype(np.float32)).astype(jnp.bfloat16)
    return high, low


SCALED = np.array(
    [
        [-6.09375, 6.8125, -4.875, 1.421875, -0.609375],
        [-1.703125, 0.0, 3.59375, -0.8671875, 0.35546875],
        [0.609375, -1.796875, 0.0, 1.796875, -0.609375],
        [-0.35546875, 0.8671875, -3.59375, 0.0, 1.703125],
        [0.609375, -1.421875, 4.875, -6.8125, 6.09375],
    ]
)


def scales():
    matrix = gll_matrix()
    equations, logs = [], []
    for a in range(5):
        for i in range(5):
            if a != i or a in (0, 4):
                equation = np.zeros(10)
                equation[a] = equation[5 + i] = abs(matrix[a, i])
                equations.append(equation)
                logs.append(abs(matrix[a, i]) * np.log(SCALED[a, i] / matrix[a, i]))
    fitted = np.linalg.lstsq(np.array(equations), np.array(logs), rcond=None)[0]
    return np.exp(fitted[:5]), np.exp(fitted[5:])


def operator_matrices():
    eye = np.eye(5)

    def along(small):
        full = np.zeros((3, LANES, LANES))
        full[0, :NPE, :NPE] = np.kron(np.kron(small, eye), eye)
        full[1, :NPE, :NPE] = np.kron(np.kron(eye, small), eye)
        full[2, :NPE, :NPE] = np.kron(np.kron(eye, eye), small)
        return full

    first = np.concatenate([full.T for full in along(SCALED)], axis=1).astype(jnp.bfloat16)
    first = np.concatenate([first, first], axis=0)
    second = np.concatenate(list(along(SCALED)), axis=0).astype(jnp.bfloat16)
    second = np.concatenate([second, second], axis=0)
    square = np.concatenate(list(along(SCALED * SCALED)), axis=0)
    third = np.concatenate(split_numpy(square), axis=1)
    third = np.concatenate([third, third], axis=0)
    row, column = scales()
    of_flux = np.zeros((1, 3 * LANES), np.float32)
    for axis in range(3):
        factors = [column, column, column]
        factors[axis] = 1.0 / row
        product = np.kron(np.kron(factors[0], factors[1]), factors[2])
        of_flux[0, axis * LANES : axis * LANES + NPE] = product * product
    of_value = np.zeros((1, LANES), np.float32)
    of_value[0, :NPE] = 1.0 / np.kron(np.kron(column, column), column)
    return first, second, third, of_flux, of_value


def split(value):
    high = value.astype(BF16)
    return high, (value - high.astype(F32)).astype(BF16)


def parts(value):
    return jnp.concatenate(split(value), axis=1)


def matmul(left, right):
    return lax.dot_general(left, right, (((1,), (0,)), ((), ())), preferred_element_type=F32)


def matmul_nt(left, right):
    return lax.dot_general(left, right, (((1,), (1,)), ((), ())), preferred_element_type=F32)


def flipped(rank, bit):
    return rank + bit - 2 * bit * ((rank // bit) % 2)


def kernel(
    devices,
    density,
    peer_rank,
    right_in,
    stiffness_in,
    mass_in,
    region_in,
    nodes_in,
    send_in,
    first_in,
    second_in,
    third_in,
    of_flux,
    of_value,
    solution_out,
    residual_out,
    right,
    stiffness,
    mass,
    region,
    nodes,
    send_nodes,
    first,
    second,
    third,
    in_sem,
    stiff,
    mass_term,
    node_table,
    key_table,
    hot,
    ghost_hot,
    results,
    diag_term,
    diagonal,
    z_own,
    w_own,
    q_own,
    p_own,
    lane_hot,
    back_hot,
    same_hot,
    diag_rows,
    ghost,
    compact,
    outgoing,
    incoming_0,
    incoming_1,
    incoming_2,
    incoming_3,
    incoming_4,
    aligned,
    edge_values,
    send_sem,
    recv_sem,
    partial,
    near_in,
    far_in,
    near_send,
    near_recv,
    far_send,
    far_recv,
):
    me = lax.axis_index("dom")

    def tile(pair):
        return slice(None), pl.ds(pl.multiple_of(pair * LANES, LANES), LANES)

    incoming = [incoming_0, incoming_1, incoming_2, incoming_3, incoming_4]
    elems = nodes.shape[1]
    pairs = elems // 2
    edge_pairs = pairs // 2
    peers = send_nodes.shape[0]
    live = peers * LANES
    run = live // edge_pairs
    bits = devices.bit_length() - 1
    candidates = [(me + 1) % devices, (me + devices - 1) % devices]
    candidates += [flipped(me, 2**k) for k in range(1, bits)]
    arrival = [1, 0] + list(range(2, len(candidates)))
    far_count = devices // GROUP
    near = [me - me % GROUP + (me + step) % GROUP for step in range(1, GROUP)]
    far = [(me + step * GROUP) % devices for step in range(1, far_count)]

    sources = [send_in, nodes_in, stiffness_in, region_in, mass_in, third_in, right_in, first_in, second_in]
    places = [send_nodes, nodes, stiffness, region, mass, third, right, first, second]
    loads = [
        pltpu.make_async_copy(source, place, in_sem.at[index])
        for index, (source, place) in enumerate(zip(sources, places))
    ]
    for load in loads:
        load.start()

    barrier = pltpu.get_barrier_semaphore()
    for other in candidates + near + far:
        pl.semaphore_signal(barrier, inc=1, device_id=(other,), device_id_type=MESH)

    loads[0].wait()
    send_row = jnp.concatenate([send_nodes[p] for p in range(peers)], axis=1)
    send_window = jnp.broadcast_to(send_row // LANES, (NV, live))
    lane_number = lax.broadcasted_iota(jnp.int32, (LANES, live), 0)
    picks = (lane_number == (send_row & (LANES - 1))).astype(F32).astype(BF16)
    lane_hot[:LANES] = picks
    lane_hot[LANES:] = picks
    lane_number = lax.broadcasted_iota(jnp.int32, (LANES, LANES), 1)
    for p in range(peers):
        column = jnp.broadcast_to(send_nodes[p], (LANES, LANES)).T
        rows = slice(p * LANES, (p + 1) * LANES)
        back_hot[rows] = (lane_number == (column & (LANES - 1))).astype(F32).astype(BF16)
        for other in range(peers):
            same_hot[rows, other * LANES : (other + 1) * LANES] = (
                (column == send_nodes[other]).astype(F32).astype(BF16)
            )
    own_count = pairs * LANES
    value_scale = of_value[...]

    def tables(half):
        columns = slice(half * LANES, (half + 1) * LANES)
        node_table[columns] = jnp.zeros((LANES, LANES), jnp.int32)
        node_table[columns, :NPE] = nodes[:, columns].T
        table = node_table[columns]
        pair_of = half * (LANES // 2) + lax.broadcasted_iota(jnp.int32, table.shape, 0) // 2
        key = jnp.where(
            table < own_count, table & (LANES - 1), LANES + ((table - run * pair_of) & (LANES - 1))
        )
        key_table[columns] = jnp.where(
            lax.broadcasted_iota(jnp.int32, table.shape, 1) < NPE, key, 255
        ).astype(F32)
        stiff[columns] = jnp.zeros((LANES, 3 * LANES), F32)
        mass_term[columns] = jnp.zeros((LANES, LANES), F32)
        for axis in range(3):
            at = slice(axis * LANES, axis * LANES + NPE)
            stiff[columns, at] = stiffness[axis, :, columns].T * of_flux[:, at]
        tag = region[:, columns]
        weight = jnp.where(tag == 0, density[0], jnp.where(tag == 1, density[1], density[2]))
        mass_term[columns, :NPE] = (mass[:, columns] * weight).T
        diag_out = matmul(parts(stiff[columns]), third[...])
        diag_term[columns] = (diag_out[:, :LANES] + diag_out[:, LANES:]) * (
            value_scale * value_scale
        ) + mass_term[columns]

    ghost[...] = jnp.zeros_like(ghost)
    for load in loads[1:6]:
        load.wait()
    tables(0)

    def scatter_rows(both, where):
        rows = jnp.concatenate([both, both - both.astype(BF16).astype(F32)], axis=0).astype(BF16)
        summed = matmul_nt(rows, where)
        return summed[:NV] + summed[NV:]

    def scatter_pair(pair, both):
        return scatter_rows(both, hot[pair])

    def gather_ghosts():
        sums = [jnp.zeros((NV, LANES), F32) for _ in range(peers)]
        lane = lax.broadcasted_iota(jnp.int32, (NV, LANES), 1)
        for pair in range(edge_pairs):
            base = pair * run
            begin = base % LANES
            row = ghost[pair]
            if begin:
                row = pltpu.roll(row, begin, 1)
            here, last = base // LANES, (base + run - 1) // LANES
            if here == last:
                sums[here] = sums[here] + row
            else:
                sums[here] = sums[here] + jnp.where(lane >= begin, row, 0.0)
                sums[last] = sums[last] + jnp.where(lane < begin, row, 0.0)
        return sums

    def remote(phase, j):
        return pltpu.make_async_remote_copy(
            src_ref=outgoing.at[phase, j],
            dst_ref=incoming[phase].at[arrival[j]],
            send_sem=send_sem.at[phase, j],
            recv_sem=recv_sem.at[phase, arrival[j]],
            device_id=(candidates[j],),
            device_id_type=MESH,
        )

    def slot_of(j):
        slot = jnp.int32(0)
        for p in range(peers):
            slot = jnp.where(peer_rank[0, p] == candidates[j], p, slot)
        return slot

    def candidate_of(p):
        found = jnp.int32(0)
        for j in range(len(candidates)):
            found = jnp.where(peer_rank[0, p] == candidates[j], j, found)
        return found

    slots_of = [slot_of(j) for j in range(len(candidates))]
    candidates_of = [candidate_of(p) for p in range(peers)]

    def send(phase, slot_values):
        for p in range(peers):
            compact[phase, p] = slot_values[p]
        for j in range(len(candidates)):
            outgoing[phase, j] = compact[phase, slots_of[j]]
            remote(phase, j).start()

    def receive(phase):
        for j in range(len(candidates)):
            remote(phase, j).wait_recv()
        return [incoming[phase][candidates_of[p]] for p in range(peers)]

    def add_returned(own, received):
        value = jnp.concatenate(received, axis=1)
        high = value.astype(BF16).astype(F32)
        low = jnp.concatenate([value - high] * 2, axis=0).astype(BF16)
        high = jnp.concatenate([high] * 2, axis=0).astype(BF16)
        window = jnp.broadcast_to((send_row // LANES).astype(F32), (2 * NV, live)).astype(BF16)
        second_row = lax.broadcasted_iota(jnp.int32, (2 * NV, live), 0) // NV
        none = jnp.zeros((2 * NV, live), BF16)

        def body(block, carry):
            high_rows, low_rows = [], []
            for i in range(WIDE // 2):
                number = (second_row + (block * WIDE + 2 * i)).astype(F32).astype(BF16)
                found = window == number
                high_rows.append(jnp.where(found, high, none))
                low_rows.append(jnp.where(found, low, none))
            summed = matmul(jnp.concatenate(high_rows + low_rows, axis=0), back_hot[...])
            summed = summed[: WIDE * NV] + summed[WIDE * NV :]
            for i in range(WIDE):
                at = tile(block * WIDE + i)
                own[at] = own[at] + summed[i * NV : (i + 1) * NV]
            return carry

        lax.fori_loop(0, pairs // WIDE, body, 0)

    def pick_shared(own):
        def body(block, total):
            rows = jnp.concatenate([own[tile(block * PICK + i)] for i in range(PICK)], axis=0)
            spread = matmul(parts(rows), lane_hot[...])
            for i in range(PICK):
                total = total + jnp.where(
                    send_window == block * PICK + i, spread[i * NV : (i + 1) * NV], 0.0
                )
            return total

        return lax.fori_loop(0, pairs // PICK, body, jnp.zeros((NV, live), F32))

    def pick_diagonal():
        spread = matmul(parts(diag_rows[...]), lane_hot[...])
        number = lax.broadcasted_iota(jnp.int32, (pairs, live), 0)
        found = jnp.where(number == send_row // LANES, spread, 0.0)
        return jnp.broadcast_to(jnp.sum(found, axis=0, keepdims=True), (NV, live))

    def add_shared(shared, received):
        value = jnp.concatenate(received, axis=1)
        rows = jnp.concatenate([value, value - value.astype(BF16).astype(F32)], axis=0).astype(BF16)
        summed = matmul(rows, same_hot[...])
        return shared + (summed[:NV] + summed[NV:])

    def slots(value):
        return [value[:, p * LANES : (p + 1) * LANES] for p in range(peers)]

    row_of = lax.broadcasted_iota(jnp.int32, (16, 2 * LANES), 0)
    one, none = jnp.ones((16, 2 * LANES), BF16), jnp.zeros((16, 2 * LANES), BF16)

    def keys_of(pair):
        both = pl.ds(2 * pair, 1), pl.ds(2 * pair + 1, 1)
        keys = jnp.concatenate([key_table[both[0], :], key_table[both[1], :]], axis=1)
        return jnp.broadcast_to(keys, (16, 2 * LANES)).astype(BF16)

    def diag_of(pair):
        both = pl.ds(2 * pair, 1), pl.ds(2 * pair + 1, 1)
        term = jnp.concatenate([diag_term[both[0], :], diag_term[both[1], :]], axis=1)
        return jnp.broadcast_to(term, (NV, 2 * LANES))

    def strip(keys, begin):
        number = (row_of + begin).astype(F32).astype(BF16)
        return jnp.where(keys == number, one, none)

    def build_ghosts():
        def body(pair, carry):
            where = strip(keys_of(pair), LANES)
            ghost_hot[pair] = where
            ghost[pair, :, : KEYS - LANES] = scatter_rows(diag_of(pair), where)
            return carry

        lax.fori_loop(0, edge_pairs, body, 0, unroll=8)

    def build_owned():
        def body(pair, carry):
            keys = keys_of(pair)
            for begin in range(0, LANES, 16):
                hot[pair, begin : begin + 16] = strip(keys, begin)
            summed = scatter_pair(pair, diag_of(pair))
            diagonal[tile(pair)] = summed
            diag_rows[pl.ds(pair, 1), :] = summed[:1]
            return carry

        lax.fori_loop(0, pairs, body, 0, unroll=4)

    def gather_pair(source, pair):
        own = source[tile(pair)]
        gathered = []
        for side in range(2):
            node = jnp.broadcast_to(node_table[pl.ds(2 * pair + side, 1), :], (NV, LANES))
            picked = jnp.take_along_axis(
                own, node & (LANES - 1), axis=1, mode="promise_in_bounds"
            )
            gathered.append(jnp.where(node < own_count, picked, 0.0))
        return gathered

    def gather_edge(source):
        def body(pair, carry):
            edge_values[pair] = jnp.concatenate(gather_pair(source, pair), axis=0)
            return carry

        lax.fori_loop(0, edge_pairs, body, 0, unroll=16)

    def apply_blocks(source, target, begin_block, end_block, total):
        edge = begin_block < edge_pairs // BLOCK

        def body(block, total):
            gathered = []
            for i in range(BLOCK):
                pair = block * BLOCK + i
                if edge:
                    spread = matmul(aligned[pair][:, : KEYS - LANES], ghost_hot[pair])
                    spread = spread[:NV] + spread[NV:]
                    gathered.append(edge_values[pair, :NV] + spread[:, :LANES])
                    gathered.append(edge_values[pair, NV:] + spread[:, LANES:])
                else:
                    gathered += gather_pair(source, pair)
            value = jnp.concatenate(gathered, axis=0)
            flux = matmul(parts(value * value_scale), first[...])
            scaled = []
            masses = []
            for i in range(2 * BLOCK):
                at = pl.ds(block * 2 * BLOCK + i, 1)
                scaled.append(flux[i * NV : (i + 1) * NV] * stiff[at, :])
                masses.append(jnp.broadcast_to(mass_term[at, :], (NV, LANES)))
            back = matmul(parts(jnp.concatenate(scaled, axis=0)), second[...])
            result = back * value_scale + jnp.concatenate(masses, axis=0) * value
            product = value * result
            for i in range(2 * BLOCK):
                total = total + product[i * NV : (i + 1) * NV]
            for i in range(BLOCK):
                pair = block * BLOCK + i
                low = 2 * i * NV
                both = jnp.concatenate(
                    [result[low : low + NV], result[low + NV : low + 2 * NV]], axis=1
                )
                if edge:
                    results[pair] = both
                    ghost[pair, :, : KEYS - LANES] = scatter_rows(both, ghost_hot[pair])
                else:
                    target[tile(pair)] = scatter_pair(pair, both)
            return total

        return lax.fori_loop(begin_block, end_block, body, total)

    def place_edge(target):
        def body(pair, carry):
            target[tile(pair)] = scatter_pair(pair, results[pair])
            return carry

        lax.fori_loop(0, edge_pairs, body, 0, unroll=8)

    def over_pairs(step, total):
        def body(pair, total):
            return step(tile(pair), total)

        return lax.fori_loop(0, pairs, body, total, unroll=8)

    zero = jnp.zeros((NV, LANES), F32)
    build_ghosts()
    pl.semaphore_wait(barrier, len(candidates) + len(near) + len(far))
    send(0, gather_ghosts())

    tables(1)
    build_owned()
    for load in loads[6:]:
        load.wait()
    right_shared = pick_shared(right)
    diag_shared = pick_diagonal()
    received = receive(0)
    diag_shared = add_shared(diag_shared, received)
    send(1, slots(right_shared / diag_shared))
    add_returned(diagonal, received)

    def begin(at, total):
        value = right[at]
        scaled = value / diagonal[at]
        z_own[at] = scaled
        return total + value * scaled

    sum_rz = over_pairs(begin, zero)
    blocks = pairs // BLOCK
    edge_blocks = edge_pairs // BLOCK
    early = edge_blocks + (blocks - edge_blocks) // 2

    def order(phase):
        received = receive(phase)
        lane = lax.broadcasted_iota(jnp.int32, (NV, LANES), 1)
        for pair in range(edge_pairs):
            start = pair * run % LANES
            here, last = pair * run // LANES, (pair * run + run - 1) // LANES
            row = received[here]
            if here != last:
                row = jnp.where(lane >= start, row, received[last])
            if start:
                row = pltpu.roll(row, LANES - start, 1)
            aligned[pair] = jnp.concatenate(
                [row, row - row.astype(BF16).astype(F32)], axis=0
            ).astype(BF16)

    gather_edge(z_own)
    sum_zw = apply_blocks(z_own, w_own, edge_blocks, early, zero)
    order(1)
    sum_zw = apply_blocks(z_own, w_own, 0, edge_blocks, sum_zw)
    send(2, gather_ghosts())
    place_edge(w_own)
    sum_zw = apply_blocks(z_own, w_own, early, blocks, sum_zw)
    image_shared = pick_shared(w_own)
    received = receive(2)
    image_shared = add_shared(image_shared, received)
    send(3, slots(image_shared / diag_shared))
    add_returned(w_own, received)

    def middle(at, total):
        value = w_own[at]
        scaled = value / diagonal[at]
        q_own[at] = scaled
        return total + value * scaled

    sum_wq = over_pairs(middle, zero)
    gather_edge(q_own)
    sum_qp = apply_blocks(q_own, p_own, edge_blocks, blocks, zero)
    order(3)
    sum_qp = apply_blocks(q_own, p_own, 0, edge_blocks, sum_qp)
    send(4, gather_ghosts())

    lane = lax.broadcasted_iota(jnp.int32, (NV, LANES), 1)
    quarter = LANES // 4
    packed = zero
    for place, total in enumerate((sum_rz, sum_zw, sum_wq, sum_qp)):
        total = total + pltpu.roll(total, LANES // 2, 1)
        total = total + pltpu.roll(total, quarter, 1)
        packed = jnp.where(lane // quarter == place, total, packed)

    def near_copy(step):
        return pltpu.make_async_remote_copy(
            src_ref=partial.at[0],
            dst_ref=near_in.at[step],
            send_sem=near_send.at[step],
            recv_sem=near_recv.at[step],
            device_id=(near[step],),
            device_id_type=MESH,
        )

    def far_copy(step):
        return pltpu.make_async_remote_copy(
            src_ref=partial.at[1],
            dst_ref=far_in.at[step],
            send_sem=far_send.at[step],
            recv_sem=far_recv.at[step],
            device_id=(far[step],),
            device_id_type=MESH,
        )

    partial[0] = packed
    for step in range(len(near)):
        near_copy(step).start()
    place_edge(p_own)
    for step in range(len(near)):
        near_copy(step).wait_recv()
        packed = packed + near_in[step]
    partial[1] = packed
    for step in range(len(far)):
        far_copy(step).start()
    add_returned(p_own, receive(4))
    for step in range(len(far)):
        far_copy(step).wait_recv()
        packed = packed + far_in[step]
    rz, zw, wq, qp = [
        jnp.sum(jnp.where(lane // quarter == place, packed, 0.0), axis=1, keepdims=True)
        for place in range(4)
    ]
    alpha = rz / zw
    new = rz - 2.0 * alpha * zw + alpha * alpha * wq
    ratio = 1.0 + new / rz
    second_alpha = new / (
        ratio * ratio * zw - 2.0 * alpha * ratio * wq + alpha * alpha * qp
    )
    outer = jnp.broadcast_to(alpha + second_alpha * ratio, (NV, LANES))
    inner = jnp.broadcast_to(alpha * second_alpha, (NV, LANES))

    def finish(at, total):
        solution_out[at] = outer * z_own[at] - inner * q_own[at]
        residual_out[at] = right[at] - outer * w_own[at] + inner * p_own[at]
        return total

    over_pairs(finish, zero)
    for phase in range(5):
        for j in range(len(candidates)):
            remote(phase, j).wait_send()
    for step in range(len(near)):
        near_copy(step).wait_send()
    for step in range(len(far)):
        far_copy(step).wait_send()


def on_device(devices, right, stiffness, mass, region, density, elem_nodes, peer_rank, send_nodes):
    first, second, third, of_flux, of_value = (
        jnp.asarray(matrix) for matrix in operator_matrices()
    )
    own_count = right.shape[1]
    elems = elem_nodes.shape[1]
    pairs = elems // 2
    peers = send_nodes.shape[1]
    live = peers * LANES
    bits = devices.bit_length() - 1
    ways = bits + 1
    near_count, far_count = GROUP - 1, devices // GROUP - 1
    vmem = pl.BlockSpec(memory_space=pltpu.VMEM)
    smem = pl.BlockSpec(memory_space=pltpu.SMEM)
    hbm = pl.BlockSpec(memory_space=pltpu.HBM)
    owned = pltpu.VMEM((NV, own_count), F32)
    dma = pltpu.SemaphoreType.DMA
    return pl.pallas_call(
        functools.partial(kernel, devices),
        out_shape=(jax.ShapeDtypeStruct((NV, own_count), F32),) * 2,
        in_specs=[smem, smem] + [hbm] * 9 + [vmem] * 2,
        out_specs=(vmem, vmem),
        scratch_shapes=[
            pltpu.VMEM((NV, own_count), F32),
            pltpu.VMEM(stiffness.shape, F32),
            pltpu.VMEM(mass.shape, F32),
            pltpu.VMEM((1, elems), jnp.int32),
            pltpu.VMEM(elem_nodes.shape, jnp.int32),
            pltpu.VMEM((peers, 1, LANES), jnp.int32),
            pltpu.VMEM(first.shape, BF16),
            pltpu.VMEM(second.shape, BF16),
            pltpu.VMEM(third.shape, BF16),
            dma((9,)),
            pltpu.VMEM((elems, 3 * LANES), F32),
            pltpu.VMEM((elems, LANES), F32),
            pltpu.VMEM((elems, LANES), jnp.int32),
            pltpu.VMEM((elems, LANES), F32),
            pltpu.VMEM((pairs, LANES, 2 * LANES), BF16),
            pltpu.VMEM((pairs // 2, KEYS - LANES, 2 * LANES), BF16),
            pltpu.VMEM((pairs // 2, NV, 2 * LANES), F32),
            pltpu.VMEM((elems, LANES), F32),
            owned,
            owned,
            owned,
            owned,
            owned,
            pltpu.VMEM((2 * LANES, live), BF16),
            pltpu.VMEM((live, LANES), BF16),
            pltpu.VMEM((live, live), BF16),
            pltpu.VMEM((pairs, LANES), F32),
            pltpu.VMEM((pairs // 2, NV, LANES), F32),
            pltpu.VMEM((5, peers, NV, LANES), F32),
            pltpu.VMEM((5, ways, NV, LANES), F32),
            pltpu.VMEM((ways, NV, LANES), F32),
            pltpu.VMEM((ways, NV, LANES), F32),
            pltpu.VMEM((ways, NV, LANES), F32),
            pltpu.VMEM((ways, NV, LANES), F32),
            pltpu.VMEM((ways, NV, LANES), F32),
            pltpu.VMEM((pairs // 2, 2 * NV, LANES), BF16),
            pltpu.VMEM((pairs // 2, 2 * NV, LANES), F32),
            dma((5, ways)),
            dma((5, ways)),
            pltpu.VMEM((2, NV, LANES), F32),
            pltpu.VMEM((near_count, NV, LANES), F32),
            pltpu.VMEM((far_count, NV, LANES), F32),
            dma((near_count,)),
            dma((near_count,)),
            dma((far_count,)),
            dma((far_count,)),
        ],
        compiler_params=pltpu.CompilerParams(
            collective_id=0, has_side_effects=True, vmem_limit_bytes=60 * 1024 * 1024
        ),
    )(
        density,
        peer_rank,
        right,
        stiffness,
        mass,
        region.reshape(1, elems),
        elem_nodes,
        jnp.transpose(send_nodes, (1, 0, 2)),
        first,
        second,
        third,
        of_flux,
        of_value,
    )


def solution(mesh):
    devices = mesh.shape["dom"]
    placed = (
        P(None, "dom"),
        P(None, None, "dom"),
        P(None, "dom"),
        P("dom"),
        P(),
        P(None, "dom"),
        P("dom", None),
        P("dom", None, None),
    )
    return jax.shard_map(
        functools.partial(on_device, devices),
        mesh=mesh,
        in_specs=placed,
        out_specs=(P(None, "dom"), P(None, "dom")),
        check_vma=False,
    )
```

```python
import functools

import jax
import jax.numpy as jnp
import numpy as np
from jax import lax
from jax.experimental import pallas as pl
from jax.experimental.pallas import tpu as pltpu
from jax.sharding import PartitionSpec as P

MESH = pl.DeviceIdType.MESH
F32 = jnp.float32
BF16 = jnp.bfloat16
NV = 8
NPE = 125
LANES = 128
GROUP = 8
KEYS = 144
BLOCK = 32
WIDE = 32
PICK = 64


def gll_matrix():
    points = np.array([-1.0, -np.sqrt(3.0 / 7.0), 0.0, np.sqrt(3.0 / 7.0), 1.0])
    weights = np.array(
        [
            1.0 / np.prod([points[column] - points[other] for other in range(5) if other != column])
            for column in range(5)
        ]
    )
    matrix = np.zeros((5, 5))
    for row_index in range(5):
        for column in range(5):
            if row_index != column:
                matrix[row_index, column] = (
                    weights[column] / weights[row_index] / (points[row_index] - points[column])
                )
        matrix[row_index, row_index] = -np.sum(matrix[row_index])
    return matrix


def split_numpy(matrix):
    single = matrix.astype(np.float32)
    high = single.astype(jnp.bfloat16)
    low = (single - high.astype(np.float32)).astype(jnp.bfloat16)
    return high, low


SCALED = np.array(
    [
        [-6.09375, 6.8125, -4.875, 1.421875, -0.609375],
        [-1.703125, 0.0, 3.59375, -0.8671875, 0.35546875],
        [0.609375, -1.796875, 0.0, 1.796875, -0.609375],
        [-0.35546875, 0.8671875, -3.59375, 0.0, 1.703125],
        [0.609375, -1.421875, 4.875, -6.8125, 6.09375],
    ]
)


def scales():
    matrix = gll_matrix()
    equations, logs = [], []
    for a in range(5):
        for i in range(5):
            if a != i or a in (0, 4):
                equation = np.zeros(10)
                equation[a] = equation[5 + i] = abs(matrix[a, i])
                equations.append(equation)
                logs.append(abs(matrix[a, i]) * np.log(SCALED[a, i] / matrix[a, i]))
    fitted = np.linalg.lstsq(np.array(equations), np.array(logs), rcond=None)[0]
    return np.exp(fitted[:5]), np.exp(fitted[5:])


def operator_matrices():
    eye = np.eye(5)

    def along(small):
        full = np.zeros((3, LANES, LANES))
        full[0, :NPE, :NPE] = np.kron(np.kron(small, eye), eye)
        full[1, :NPE, :NPE] = np.kron(np.kron(eye, small), eye)
        full[2, :NPE, :NPE] = np.kron(np.kron(eye, eye), small)
        return full

    first = np.concatenate([full.T for full in along(SCALED)], axis=1).astype(jnp.bfloat16)
    first = np.concatenate([first, first], axis=0)
    second = np.concatenate(list(along(SCALED)), axis=0).astype(jnp.bfloat16)
    second = np.concatenate([second, second], axis=0)
    square = np.concatenate(list(along(SCALED * SCALED)), axis=0)
    third = np.concatenate(split_numpy(square), axis=1)
    third = np.concatenate([third, third], axis=0)
    row, column = scales()
    of_flux = np.zeros((1, 3 * LANES), np.float32)
    for axis in range(3):
        factors = [column, column, column]
        factors[axis] = 1.0 / row
        product = np.kron(np.kron(factors[0], factors[1]), factors[2])
        of_flux[0, axis * LANES : axis * LANES + NPE] = product * product
    of_value = np.zeros((1, LANES), np.float32)
    of_value[0, :NPE] = 1.0 / np.kron(np.kron(column, column), column)
    return first, second, third, of_flux, of_value


def split(value):
    high = value.astype(BF16)
    return high, (value - high.astype(F32)).astype(BF16)


def parts(value):
    return jnp.concatenate(split(value), axis=1)


def matmul(left, right):
    return lax.dot_general(left, right, (((1,), (0,)), ((), ())), preferred_element_type=F32)


def matmul_nt(left, right):
    return lax.dot_general(left, right, (((1,), (1,)), ((), ())), preferred_element_type=F32)


def flipped(rank, bit):
    return rank + bit - 2 * bit * ((rank // bit) % 2)


def kernel(
    devices,
    density,
    peer_rank,
    right_in,
    stiffness_in,
    mass_in,
    region_in,
    nodes_in,
    send_in,
    first_in,
    second_in,
    third_in,
    of_flux,
    of_value,
    solution_out,
    residual_out,
    right,
    stiffness,
    mass,
    region,
    nodes,
    send_nodes,
    first,
    second,
    third,
    in_sem,
    stiff,
    mass_term,
    node_table,
    key_table,
    hot,
    ghost_hot,
    results,
    diag_term,
    diagonal,
    z_own,
    w_own,
    q_own,
    p_own,
    lane_hot,
    back_hot,
    same_hot,
    diag_rows,
    ghost,
    compact,
    outgoing,
    incoming_0,
    incoming_1,
    incoming_2,
    incoming_3,
    incoming_4,
    aligned,
    edge_values,
    flux_parts,
    send_sem,
    recv_sem,
    partial,
    near_in,
    far_in,
    near_send,
    near_recv,
    far_send,
    far_recv,
):
    me = lax.axis_index("dom")

    def tile(pair):
        return slice(None), pl.ds(pl.multiple_of(pair * LANES, LANES), LANES)

    incoming = [incoming_0, incoming_1, incoming_2, incoming_3, incoming_4]
    elems = nodes.shape[1]
    pairs = elems // 2
    edge_pairs = pairs // 2
    peers = send_nodes.shape[0]
    live = peers * LANES
    run = live // edge_pairs
    bits = devices.bit_length() - 1
    candidates = [(me + 1) % devices, (me + devices - 1) % devices]
    candidates += [flipped(me, 2**k) for k in range(1, bits)]
    arrival = [1, 0] + list(range(2, len(candidates)))
    far_count = devices // GROUP
    near = [me - me % GROUP + (me + step) % GROUP for step in range(1, GROUP)]
    far = [(me + step * GROUP) % devices for step in range(1, far_count)]

    sources = [send_in, nodes_in, stiffness_in, region_in, mass_in, third_in, right_in, first_in, second_in]
    places = [send_nodes, nodes, stiffness, region, mass, third, right, first, second]
    loads = [
        pltpu.make_async_copy(source, place, in_sem.at[index])
        for index, (source, place) in enumerate(zip(sources, places))
    ]
    for load in loads:
        load.start()

    barrier = pltpu.get_barrier_semaphore()
    for other in candidates + near + far:
        pl.semaphore_signal(barrier, inc=1, device_id=(other,), device_id_type=MESH)

    loads[0].wait()
    send_row = jnp.concatenate([send_nodes[p] for p in range(peers)], axis=1)
    send_window = jnp.broadcast_to(send_row // LANES, (NV, live))
    lane_number = lax.broadcasted_iota(jnp.int32, (LANES, live), 0)
    picks = (lane_number == (send_row & (LANES - 1))).astype(F32).astype(BF16)
    lane_hot[:LANES] = picks
    lane_hot[LANES:] = picks
    lane_number = lax.broadcasted_iota(jnp.int32, (LANES, LANES), 1)
    for p in range(peers):
        column = jnp.broadcast_to(send_nodes[p], (LANES, LANES)).T
        rows = slice(p * LANES, (p + 1) * LANES)
        back_hot[rows] = (lane_number == (column & (LANES - 1))).astype(F32).astype(BF16)
        for other in range(peers):
            same_hot[rows, other * LANES : (other + 1) * LANES] = (
                (column == send_nodes[other]).astype(F32).astype(BF16)
            )
    own_count = pairs * LANES
    value_scale = of_value[...]

    def tables(half):
        columns = slice(half * LANES, (half + 1) * LANES)
        node_table[columns] = jnp.zeros((LANES, LANES), jnp.int32)
        node_table[columns, :NPE] = nodes[:, columns].T
        table = node_table[columns]
        pair_of = half * (LANES // 2) + lax.broadcasted_iota(jnp.int32, table.shape, 0) // 2
        key = jnp.where(
            table < own_count, table & (LANES - 1), LANES + ((table - run * pair_of) & (LANES - 1))
        )
        key_table[columns] = jnp.where(
            lax.broadcasted_iota(jnp.int32, table.shape, 1) < NPE, key, 255
        ).astype(F32)
        stiff[columns] = jnp.zeros((LANES, 3 * LANES), F32)
        mass_term[columns] = jnp.zeros((LANES, LANES), F32)
        for axis in range(3):
            at = slice(axis * LANES, axis * LANES + NPE)
            stiff[columns, at] = stiffness[axis, :, columns].T * of_flux[:, at]
        tag = region[:, columns]
        weight = jnp.where(tag == 0, density[0], jnp.where(tag == 1, density[1], density[2]))
        mass_term[columns, :NPE] = (mass[:, columns] * weight).T
        diag_out = matmul(parts(stiff[columns]), third[...])
        diag_term[columns] = (diag_out[:, :LANES] + diag_out[:, LANES:]) * (
            value_scale * value_scale
        ) + mass_term[columns]

    ghost[...] = jnp.zeros_like(ghost)
    for load in loads[1:6]:
        load.wait()
    tables(0)

    def scatter_rows(both, where):
        rows = jnp.concatenate([both, both - both.astype(BF16).astype(F32)], axis=0).astype(BF16)
        summed = matmul_nt(rows, where)
        return summed[:NV] + summed[NV:]

    def scatter_pair(pair, both):
        return scatter_rows(both, hot[pair])

    def gather_ghosts():
        sums = [jnp.zeros((NV, LANES), F32) for _ in range(peers)]
        lane = lax.broadcasted_iota(jnp.int32, (NV, LANES), 1)
        for pair in range(edge_pairs):
            base = pair * run
            begin = base % LANES
            row = ghost[pair]
            if begin:
                row = pltpu.roll(row, begin, 1)
            here, last = base // LANES, (base + run - 1) // LANES
            if here == last:
                sums[here] = sums[here] + row
            else:
                sums[here] = sums[here] + jnp.where(lane >= begin, row, 0.0)
                sums[last] = sums[last] + jnp.where(lane < begin, row, 0.0)
        return sums

    def remote(phase, j):
        return pltpu.make_async_remote_copy(
            src_ref=outgoing.at[phase, j],
            dst_ref=incoming[phase].at[arrival[j]],
            send_sem=send_sem.at[phase, j],
            recv_sem=recv_sem.at[phase, arrival[j]],
            device_id=(candidates[j],),
            device_id_type=MESH,
        )

    def slot_of(j):
        slot = jnp.int32(0)
        for p in range(peers):
            slot = jnp.where(peer_rank[0, p] == candidates[j], p, slot)
        return slot

    def candidate_of(p):
        found = jnp.int32(0)
        for j in range(len(candidates)):
            found = jnp.where(peer_rank[0, p] == candidates[j], j, found)
        return found

    slots_of = [slot_of(j) for j in range(len(candidates))]
    candidates_of = [candidate_of(p) for p in range(peers)]

    def send(phase, slot_values):
        for p in range(peers):
            compact[phase, p] = slot_values[p]
        for j in range(len(candidates)):
            outgoing[phase, j] = compact[phase, slots_of[j]]
            remote(phase, j).start()

    def receive(phase):
        for j in range(len(candidates)):
            remote(phase, j).wait_recv()
        return [incoming[phase][candidates_of[p]] for p in range(peers)]

    def add_returned(own, received):
        value = jnp.concatenate(received, axis=1)
        high = value.astype(BF16).astype(F32)
        low = jnp.concatenate([value - high] * 2, axis=0).astype(BF16)
        high = jnp.concatenate([high] * 2, axis=0).astype(BF16)
        window = jnp.broadcast_to((send_row // LANES).astype(F32), (2 * NV, live)).astype(BF16)
        second_row = lax.broadcasted_iota(jnp.int32, (2 * NV, live), 0) // NV
        none = jnp.zeros((2 * NV, live), BF16)

        def body(block, carry):
            high_rows, low_rows = [], []
            for i in range(WIDE // 2):
                number = (second_row + (block * WIDE + 2 * i)).astype(F32).astype(BF16)
                found = window == number
                high_rows.append(jnp.where(found, high, none))
                low_rows.append(jnp.where(found, low, none))
            summed = matmul(jnp.concatenate(high_rows + low_rows, axis=0), back_hot[...])
            summed = summed[: WIDE * NV] + summed[WIDE * NV :]
            for i in range(WIDE):
                at = tile(block * WIDE + i)
                own[at] = own[at] + summed[i * NV : (i + 1) * NV]
            return carry

        lax.fori_loop(0, pairs // WIDE, body, 0)

    def pick_shared(own):
        def body(block, total):
            rows = jnp.concatenate([own[tile(block * PICK + i)] for i in range(PICK)], axis=0)
            spread = matmul(parts(rows), lane_hot[...])
            for i in range(PICK):
                total = total + jnp.where(
                    send_window == block * PICK + i, spread[i * NV : (i + 1) * NV], 0.0
                )
            return total

        return lax.fori_loop(0, pairs // PICK, body, jnp.zeros((NV, live), F32))

    def pick_diagonal():
        spread = matmul(parts(diag_rows[...]), lane_hot[...])
        number = lax.broadcasted_iota(jnp.int32, (pairs, live), 0)
        found = jnp.where(number == send_row // LANES, spread, 0.0)
        return jnp.broadcast_to(jnp.sum(found, axis=0, keepdims=True), (NV, live))

    def add_shared(shared, received):
        value = jnp.concatenate(received, axis=1)
        rows = jnp.concatenate([value, value - value.astype(BF16).astype(F32)], axis=0).astype(BF16)
        summed = matmul(rows, same_hot[...])
        return shared + (summed[:NV] + summed[NV:])

    def slots(value):
        return [value[:, p * LANES : (p + 1) * LANES] for p in range(peers)]

    row_of = lax.broadcasted_iota(jnp.int32, (16, 2 * LANES), 0)
    one, none = jnp.ones((16, 2 * LANES), BF16), jnp.zeros((16, 2 * LANES), BF16)

    def keys_of(pair):
        both = pl.ds(2 * pair, 1), pl.ds(2 * pair + 1, 1)
        keys = jnp.concatenate([key_table[both[0], :], key_table[both[1], :]], axis=1)
        return jnp.broadcast_to(keys, (16, 2 * LANES)).astype(BF16)

    def diag_of(pair):
        both = pl.ds(2 * pair, 1), pl.ds(2 * pair + 1, 1)
        term = jnp.concatenate([diag_term[both[0], :], diag_term[both[1], :]], axis=1)
        return jnp.broadcast_to(term, (NV, 2 * LANES))

    def strip(keys, begin):
        number = (row_of + begin).astype(F32).astype(BF16)
        return jnp.where(keys == number, one, none)

    def build_ghosts():
        def body(pair, carry):
            where = strip(keys_of(pair), LANES)
            ghost_hot[pair] = where
            ghost[pair, :, : KEYS - LANES] = scatter_rows(diag_of(pair), where)
            return carry

        lax.fori_loop(0, edge_pairs, body, 0, unroll=8)

    def build_owned():
        def body(pair, carry):
            keys = keys_of(pair)
            for begin in range(0, LANES, 16):
                hot[pair, begin : begin + 16] = strip(keys, begin)
            summed = scatter_pair(pair, diag_of(pair))
            diagonal[tile(pair)] = summed
            diag_rows[pl.ds(pair, 1), :] = summed[:1]
            return carry

        lax.fori_loop(0, pairs, body, 0, unroll=4)

    def gather_pair(source, pair):
        own = source[tile(pair)]
        gathered = []
        for side in range(2):
            node = jnp.broadcast_to(node_table[pl.ds(2 * pair + side, 1), :], (NV, LANES))
            picked = jnp.take_along_axis(
                own, node & (LANES - 1), axis=1, mode="promise_in_bounds"
            )
            gathered.append(jnp.where(node < own_count, picked, 0.0))
        return gathered

    def gather_edge(source):
        def body(pair, carry):
            edge_values[pair] = jnp.concatenate(gather_pair(source, pair), axis=0)
            return carry

        lax.fori_loop(0, edge_pairs, body, 0, unroll=16)

    def apply_blocks(source, target, begin_block, end_block, total):
        edge = begin_block < edge_pairs // BLOCK

        def body(block, total):
            gathered = []
            for i in range(BLOCK):
                pair = block * BLOCK + i
                if edge:
                    spread = matmul(aligned[pair][:, : KEYS - LANES], ghost_hot[pair])
                    spread = spread[:NV] + spread[NV:]
                    gathered.append(edge_values[pair, :NV] + spread[:, :LANES])
                    gathered.append(edge_values[pair, NV:] + spread[:, LANES:])
                else:
                    gathered += gather_pair(source, pair)
            value = jnp.concatenate(gathered, axis=0)
            flux = matmul(parts(value * value_scale), first[...])
            scaled = []
            masses = []
            for i in range(2 * BLOCK):
                at = pl.ds(block * 2 * BLOCK + i, 1)
                scaled.append(flux[i * NV : (i + 1) * NV] * stiff[at, :])
                masses.append(jnp.broadcast_to(mass_term[at, :], (NV, LANES)))
            back = matmul(parts(jnp.concatenate(scaled, axis=0)), second[...])
            result = back * value_scale + jnp.concatenate(masses, axis=0) * value
            product = value * result
            for i in range(2 * BLOCK):
                total = total + product[i * NV : (i + 1) * NV]
            for i in range(BLOCK):
                pair = block * BLOCK + i
                low = 2 * i * NV
                both = jnp.concatenate(
                    [result[low : low + NV], result[low + NV : low + 2 * NV]], axis=1
                )
                if edge:
                    results[pair] = both
                    ghost[pair, :, : KEYS - LANES] = scatter_rows(both, ghost_hot[pair])
                else:
                    target[tile(pair)] = scatter_pair(pair, both)
            return total

        return lax.fori_loop(begin_block, end_block, body, total)

    def edge_energy(total):
        def body(block, total):
            gathered, scaled = [], []
            for i in range(BLOCK):
                pair = block * BLOCK + i
                spread = matmul(aligned[pair][:, : KEYS - LANES], ghost_hot[pair])
                spread = spread[:NV] + spread[NV:]
                spread = jnp.concatenate([spread[:, :LANES], spread[:, LANES:]], axis=0)
                value = edge_values[pair] + spread
                edge_values[pair] = value
                gathered.append(value)
            value = jnp.concatenate(gathered, axis=0)
            flux = matmul(parts(value * value_scale), first[...])
            for i in range(2 * BLOCK):
                at = pl.ds(block * 2 * BLOCK + i, 1)
                low, high = i * NV, (i + 1) * NV
                scaled.append(flux[low:high] * stiff[at, :])
                product = scaled[-1] * flux[low:high]
                total = total + (product[:, :LANES] + product[:, LANES : 2 * LANES])
                total = total + product[:, 2 * LANES :]
                total = total + mass_term[at, :] * (value[low:high] * value[low:high])
            rows = 2 * BLOCK * NV
            at = pl.ds(pl.multiple_of(block * rows, rows), rows)
            flux_parts[at, :] = parts(jnp.concatenate(scaled, axis=0))
            return total

        return lax.fori_loop(0, edge_pairs // BLOCK, body, total)

    def edge_results():
        def body(block, carry):
            rows = 2 * BLOCK * NV
            at = pl.ds(pl.multiple_of(block * rows, rows), rows)
            back = matmul(flux_parts[at, :], second[...]) * value_scale
            for i in range(BLOCK):
                pair = block * BLOCK + i
                sides = []
                for side in range(2):
                    low = (2 * i + side) * NV
                    sides.append(
                        back[low : low + NV]
                        + mass_term[pl.ds(2 * pair + side, 1), :]
                        * edge_values[pair, side * NV : (side + 1) * NV]
                    )
                both = jnp.concatenate(sides, axis=1)
                results[pair] = both
                ghost[pair, :, : KEYS - LANES] = scatter_rows(both, ghost_hot[pair])
            return carry

        lax.fori_loop(0, edge_pairs // BLOCK, body, 0)

    def place_edge(target):
        def body(pair, carry):
            target[tile(pair)] = scatter_pair(pair, results[pair])
            return carry

        lax.fori_loop(0, edge_pairs, body, 0, unroll=8)

    def over_pairs(step, total):
        def body(pair, total):
            return step(tile(pair), total)

        return lax.fori_loop(0, pairs, body, total, unroll=8)

    zero = jnp.zeros((NV, LANES), F32)
    build_ghosts()
    pl.semaphore_wait(barrier, len(candidates) + len(near) + len(far))
    send(0, gather_ghosts())

    tables(1)
    build_owned()
    for load in loads[6:]:
        load.wait()
    right_shared = pick_shared(right)
    diag_shared = pick_diagonal()
    received = receive(0)
    diag_shared = add_shared(diag_shared, received)
    send(1, slots(right_shared / diag_shared))
    add_returned(diagonal, received)

    def begin(at, total):
        value = right[at]
        scaled = value / diagonal[at]
        z_own[at] = scaled
        return total + value * scaled

    sum_rz = over_pairs(begin, zero)
    blocks = pairs // BLOCK
    edge_blocks = edge_pairs // BLOCK
    early = edge_blocks + (blocks - edge_blocks) // 2

    def order(phase):
        received = receive(phase)
        lane = lax.broadcasted_iota(jnp.int32, (NV, LANES), 1)
        for pair in range(edge_pairs):
            start = pair * run % LANES
            here, last = pair * run // LANES, (pair * run + run - 1) // LANES
            row = received[here]
            if here != last:
                row = jnp.where(lane >= start, row, received[last])
            if start:
                row = pltpu.roll(row, LANES - start, 1)
            aligned[pair] = jnp.concatenate(
                [row, row - row.astype(BF16).astype(F32)], axis=0
            ).astype(BF16)

    gather_edge(z_own)
    sum_zw = apply_blocks(z_own, w_own, edge_blocks, early, zero)
    order(1)
    sum_zw = apply_blocks(z_own, w_own, 0, edge_blocks, sum_zw)
    send(2, gather_ghosts())
    place_edge(w_own)
    sum_zw = apply_blocks(z_own, w_own, early, blocks, sum_zw)
    image_shared = pick_shared(w_own)
    received = receive(2)
    image_shared = add_shared(image_shared, received)
    send(3, slots(image_shared / diag_shared))
    add_returned(w_own, received)

    def middle(at, total):
        value = w_own[at]
        scaled = value / diagonal[at]
        q_own[at] = scaled
        return total + value * scaled

    sum_wq = over_pairs(middle, zero)
    gather_edge(q_own)
    sum_qp = apply_blocks(q_own, p_own, edge_blocks, blocks, zero)
    order(3)
    sum_qp = edge_energy(sum_qp)

    lane = lax.broadcasted_iota(jnp.int32, (NV, LANES), 1)
    quarter = LANES // 4
    packed = zero
    for place, total in enumerate((sum_rz, sum_zw, sum_wq, sum_qp)):
        total = total + pltpu.roll(total, LANES // 2, 1)
        total = total + pltpu.roll(total, quarter, 1)
        packed = jnp.where(lane // quarter == place, total, packed)

    def near_copy(step):
        return pltpu.make_async_remote_copy(
            src_ref=partial.at[0],
            dst_ref=near_in.at[step],
            send_sem=near_send.at[step],
            recv_sem=near_recv.at[step],
            device_id=(near[step],),
            device_id_type=MESH,
        )

    def far_copy(step):
        return pltpu.make_async_remote_copy(
            src_ref=partial.at[1],
            dst_ref=far_in.at[step],
            send_sem=far_send.at[step],
            recv_sem=far_recv.at[step],
            device_id=(far[step],),
            device_id_type=MESH,
        )

    partial[0] = packed
    for step in range(len(near)):
        near_copy(step).start()
    edge_results()
    send(4, gather_ghosts())
    place_edge(p_own)
    for step in range(len(near)):
        near_copy(step).wait_recv()
        packed = packed + near_in[step]
    partial[1] = packed
    for step in range(len(far)):
        far_copy(step).start()
    add_returned(p_own, receive(4))
    for step in range(len(far)):
        far_copy(step).wait_recv()
        packed = packed + far_in[step]
    rz, zw, wq, qp = [
        jnp.sum(jnp.where(lane // quarter == place, packed, 0.0), axis=1, keepdims=True)
        for place in range(4)
    ]
    alpha = rz / zw
    new = rz - 2.0 * alpha * zw + alpha * alpha * wq
    ratio = 1.0 + new / rz
    second_alpha = new / (
        ratio * ratio * zw - 2.0 * alpha * ratio * wq + alpha * alpha * qp
    )
    outer = jnp.broadcast_to(alpha + second_alpha * ratio, (NV, LANES))
    inner = jnp.broadcast_to(alpha * second_alpha, (NV, LANES))

    def finish(at, total):
        solution_out[at] = outer * z_own[at] - inner * q_own[at]
        residual_out[at] = right[at] - outer * w_own[at] + inner * p_own[at]
        return total

    over_pairs(finish, zero)
    for phase in range(5):
        for j in range(len(candidates)):
            remote(phase, j).wait_send()
    for step in range(len(near)):
        near_copy(step).wait_send()
    for step in range(len(far)):
        far_copy(step).wait_send()


def on_device(devices, right, stiffness, mass, region, density, elem_nodes, peer_rank, send_nodes):
    first, second, third, of_flux, of_value = (
        jnp.asarray(matrix) for matrix in operator_matrices()
    )
    own_count = right.shape[1]
    elems = elem_nodes.shape[1]
    pairs = elems // 2
    peers = send_nodes.shape[1]
    live = peers * LANES
    bits = devices.bit_length() - 1
    ways = bits + 1
    near_count, far_count = GROUP - 1, devices // GROUP - 1
    vmem = pl.BlockSpec(memory_space=pltpu.VMEM)
    smem = pl.BlockSpec(memory_space=pltpu.SMEM)
    hbm = pl.BlockSpec(memory_space=pltpu.HBM)
    owned = pltpu.VMEM((NV, own_count), F32)
    dma = pltpu.SemaphoreType.DMA
    return pl.pallas_call(
        functools.partial(kernel, devices),
        out_shape=(jax.ShapeDtypeStruct((NV, own_count), F32),) * 2,
        in_specs=[smem, smem] + [hbm] * 9 + [vmem] * 2,
        out_specs=(vmem, vmem),
        scratch_shapes=[
            pltpu.VMEM((NV, own_count), F32),
            pltpu.VMEM(stiffness.shape, F32),
            pltpu.VMEM(mass.shape, F32),
            pltpu.VMEM((1, elems), jnp.int32),
            pltpu.VMEM(elem_nodes.shape, jnp.int32),
            pltpu.VMEM((peers, 1, LANES), jnp.int32),
            pltpu.VMEM(first.shape, BF16),
            pltpu.VMEM(second.shape, BF16),
            pltpu.VMEM(third.shape, BF16),
            dma((9,)),
            pltpu.VMEM((elems, 3 * LANES), F32),
            pltpu.VMEM((elems, LANES), F32),
            pltpu.VMEM((elems, LANES), jnp.int32),
            pltpu.VMEM((elems, LANES), F32),
            pltpu.VMEM((pairs, LANES, 2 * LANES), BF16),
            pltpu.VMEM((pairs // 2, KEYS - LANES, 2 * LANES), BF16),
            pltpu.VMEM((pairs // 2, NV, 2 * LANES), F32),
            pltpu.VMEM((elems, LANES), F32),
            owned,
            owned,
            owned,
            owned,
            owned,
            pltpu.VMEM((2 * LANES, live), BF16),
            pltpu.VMEM((live, LANES), BF16),
            pltpu.VMEM((live, live), BF16),
            pltpu.VMEM((pairs, LANES), F32),
            pltpu.VMEM((pairs // 2, NV, LANES), F32),
            pltpu.VMEM((5, peers, NV, LANES), F32),
            pltpu.VMEM((5, ways, NV, LANES), F32),
            pltpu.VMEM((ways, NV, LANES), F32),
            pltpu.VMEM((ways, NV, LANES), F32),
            pltpu.VMEM((ways, NV, LANES), F32),
            pltpu.VMEM((ways, NV, LANES), F32),
            pltpu.VMEM((ways, NV, LANES), F32),
            pltpu.VMEM((pairs // 2, 2 * NV, LANES), BF16),
            pltpu.VMEM((pairs // 2, 2 * NV, LANES), F32),
            pltpu.VMEM((pairs * NV, 6 * LANES), BF16),
            dma((5, ways)),
            dma((5, ways)),
            pltpu.VMEM((2, NV, LANES), F32),
            pltpu.VMEM((near_count, NV, LANES), F32),
            pltpu.VMEM((far_count, NV, LANES), F32),
            dma((near_count,)),
            dma((near_count,)),
            dma((far_count,)),
            dma((far_count,)),
        ],
        compiler_params=pltpu.CompilerParams(
            collective_id=0, has_side_effects=True, vmem_limit_bytes=60 * 1024 * 1024
        ),
    )(
        density,
        peer_rank,
        right,
        stiffness,
        mass,
        region.reshape(1, elems),
        elem_nodes,
        jnp.transpose(send_nodes, (1, 0, 2)),
        first,
        second,
        third,
        of_flux,
        of_value,
    )


def solution(mesh):
    devices = mesh.shape["dom"]
    placed = (
        P(None, "dom"),
        P(None, None, "dom"),
        P(None, "dom"),
        P("dom"),
        P(),
        P(None, "dom"),
        P("dom", None),
        P("dom", None, None),
    )
    return jax.shard_map(
        functools.partial(on_device, devices),
        mesh=mesh,
        in_specs=placed,
        out_specs=(P(None, "dom"), P(None, "dom")),
        check_vma=False,
    )
```
